512 devices in a mesh: dp: 128 (over x, y_lo, z, core), mp: 4 (over y_hi).
Axes of the slice: x: 4, y: 8 (y_hi: 4, y_lo: 2; y = y_hi * 2 + y_lo), z: 8, core: 2. Of those that a mesh axis runs over, the one named last changes fastest.
Arguments:
- images: bfloat16 [256, 256, 3136], P('dp', 'mp'), may hold values from -16 to 16
- permutation: int32 [256], replicated, may hold values from 0 to 255, as said below
- inverse: int32 [256], replicated, may hold values from 0 to 255, as said below
- reduce_weight: bfloat16 [64, 256], P(None, 'mp'), may hold values from -0.375 to 0.375
- reduce_gain: float32 [64], P('mp'), may hold values from 0.5 to 1.5
- reduce_shift: float32 [64], P('mp'), may hold values from -3 to 3
- spatial_weight: bfloat16 [64, 64, 3, 3], P('mp'), may hold values from -0.25 to 0.25
- spatial_gain: float32 [64], P('mp'), may hold values from 0.5 to 1.5
- spatial_shift: float32 [64], P('mp'), may hold values from -3 to 3
- expand_weight: bfloat16 [256, 64], P('mp'), may hold values from -0.75 to 0.75
- expand_gain: float32 [256], P('mp'), may hold values from 0.5 to 1.5
- expand_shift: float32 [256], P('mp'), may hold values from -3 to 3
- projection: bfloat16 [256, 128], P('mp'), may hold values from -0.375 to 0.375
- queries: float32 [256, 128], P('dp'), may hold values from -6 to 6
- dictionary_bank: bfloat16 [4096, 128], P('mp'), may hold values from -1.5 to 1.5
Outputs:
- features: bfloat16 [256, 256, 3136], P('dp', 'mp')
- matched_similarity_scores: float32 [256, 256], P('dp')
- loss: float32 [256], P('dp')
The draws below stay inside these ranges and needn't reach their ends.
Inputs may be any that keep to these rules, and one draw needn't show every extreme that they name: A permutation: every value of 0 to 255 once. The inverse of permutation: inverse[permutation[i]] = i.
All inputs are finite; a program needn't handle non-finite values.
Results may differ from the reference program's by a relative error of at most 0.015.
Values may be sent and summed in bfloat16 or wider, within the bound.
A program may use at most 64 MiB of HBM per device.

```python
import jax
import jax.numpy as jnp
from jax import lax

C = 256
MID = 64
EMB = 128
SIDE = 56
QUEUE = 4096
IMG_DEV = 2
IMAGES = 256
MAP_PIXEL_COUNT = 3136
N_DP = 128
N_MP = 4


def shared_order(key):
    return jax.random.permutation(key, jnp.arange(IMAGES, dtype=jnp.int32))


def draw_permutation(key, part):
    return shared_order(key)


def draw_inverse(key, part):
    ordering = shared_order(key)
    return jnp.argsort(ordering).astype(jnp.int32)


def image_field(key, lowest, highest, noise):
    scale_key, offset_key = jax.random.split(key)
    spans = jax.random.uniform(scale_key, (IMAGES, 1, 1), jnp.float32, jnp.log(lowest), jnp.log(highest))
    offsets = jax.random.normal(offset_key, (IMAGES, C, 1), jnp.float32)
    return jnp.clip(jnp.exp(spans) * (offsets + noise), -16.0, 16.0).astype(jnp.bfloat16)


def draw_images(key, part):
    key = jax.random.fold_in(key, 11)
    field_key, noise_key = jax.random.split(key)
    noise = jnp.clip(jax.random.normal(noise_key, (IMAGES, C, MAP_PIXEL_COUNT), jnp.float32), -4.0, 4.0)
    return image_field(field_key, 0.3, 3.0, noise)


def bank_rows(entries, top_norm):
    position = jnp.arange(QUEUE, dtype=jnp.float32)[:, None] / QUEUE
    row_norm = 1.0 + (top_norm - 1.0) * position
    return jnp.clip(entries * row_norm / jnp.sqrt(EMB * 1.0), -1.5, 1.5).astype(jnp.bfloat16)


def draw_dictionary_bank(key, part):
    key = jax.random.fold_in(key, 23)
    entries = jnp.clip(jax.random.normal(key, (QUEUE, EMB), jnp.float32), -4.0, 4.0)
    return bank_rows(entries, 3.5)


def shard_levels(rng, dims, pieces, smallest, top_value):
    gain, own = 1.0, jax.random.fold_in(rng, 6)
    for axis_at, shards_of in pieces:
        heights = jnp.exp(jax.random.uniform(jax.random.fold_in(own, axis_at), (shards_of,), jnp.float32, smallest / len(pieces), top_value / len(pieces)))
        gain = gain * jnp.repeat(heights, dims[axis_at] // shards_of).reshape([-1 if axis == axis_at else 1 for axis in range(len(dims))])
    return gain


def scatter_about(rng, extent, width, limit, pieces=(), kind=jnp.bfloat16):
    values = width * jax.random.normal(rng, extent, jnp.float32)
    if pieces:
        values = values * shard_levels(rng, extent, pieces, -0.22, 0.18)
    return jnp.clip(values, -limit, limit).astype(kind)


def setup_inputs(seed: int = 0) -> dict:
    keys = jax.random.split(jax.random.key(seed), 16)
    return {
        "images": draw_images(jax.random.fold_in(keys[15], 71), 0),
        "permutation": draw_permutation(jax.random.fold_in(keys[15], 71), 0),
        "inverse": draw_inverse(jax.random.fold_in(keys[15], 71), 0),
        "reduce_weight": scatter_about(keys[3], (MID, C), C ** -0.5, 0.375, ((1, 4),)),
        "reduce_gain": jnp.clip(1.0 + 0.1 * jax.random.normal(keys[4], (MID,), jnp.float32), 0.5, 1.5),
        "reduce_shift": scatter_about(keys[5], (MID,), 0.5, 3.0, ((0, 4),), jnp.float32),
        "spatial_weight": scatter_about(keys[6], (MID, MID, 3, 3), (9 * MID) ** -0.5, 0.25, ((0, 4),)),
        "spatial_gain": jnp.clip(1.0 + 0.1 * jax.random.normal(keys[7], (MID,), jnp.float32), 0.5, 1.5),
        "spatial_shift": scatter_about(keys[8], (MID,), 0.5, 3.0, ((0, 4),), jnp.float32),
        "expand_weight": scatter_about(keys[9], (C, MID), MID ** -0.5, 0.75, ((0, 4),)),
        "expand_gain": jnp.clip(1.0 + 0.1 * jax.random.normal(keys[10], (C,), jnp.float32), 0.5, 1.5),
        "expand_shift": scatter_about(keys[11], (C,), 0.5, 3.0, ((0, 4),), jnp.float32),
        "projection": scatter_about(keys[12], (C, EMB), C ** -0.5, 0.375, ((0, 4),)),
        "queries": scatter_about(keys[13], (IMAGES, EMB), 1.0, 6.0, ((0, 128),), jnp.float32),
        "dictionary_bank": draw_dictionary_bank(jax.random.fold_in(keys[15], 71), 0),
    }


sharpness_divisor = 0.2

def normalize(values, gain_vec, shift_vec):
    center = lax.optimization_barrier(jnp.mean(values, axis=(0, 2), keepdims=True))
    spread = lax.optimization_barrier(jnp.mean((values - center) ** 2, axis=(0, 2), keepdims=True))
    return (values - center) * lax.rsqrt(spread + 1e-05) * gain_vec[None, :, None] + shift_vec[None, :, None]

def reference(images, permutation, inverse, reduce_weight, reduce_gain, reduce_shift, spatial_weight, spatial_gain, spatial_shift, expand_weight, expand_gain, expand_shift, projection, queries, dictionary_bank):
    grouped = images.reshape(N_DP, IMG_DEV, C, MAP_PIXEL_COUNT)
    weight_parts = reduce_weight.astype(jnp.float32).reshape(MID, N_MP, C // N_MP)

    def reduce_group(block):
        split_in = block.astype(jnp.float32).reshape(IMG_DEV, N_MP, C // N_MP, MAP_PIXEL_COUNT)
        partial_sums = jnp.einsum('bgcp,ogc->gbop', split_in, weight_parts, precision=lax.Precision.HIGHEST)
        rounded = lax.optimization_barrier(partial_sums.astype(jnp.bfloat16)).astype(jnp.float32)
        return lax.optimization_barrier(jnp.sum(rounded, axis=0)).astype(jnp.bfloat16)
    reduced = lax.map(reduce_group, grouped).reshape(IMAGES, MID, MAP_PIXEL_COUNT)
    shuffled = jnp.take(reduced, permutation, axis=0).reshape(N_DP, IMG_DEV, MID, MAP_PIXEL_COUNT)

    def block_group(section):
        first = jnp.maximum(normalize(section.astype(jnp.float32), reduce_gain, reduce_shift), 0.0).astype(jnp.bfloat16)
        maps = first.astype(jnp.float32).reshape(IMG_DEV, MID, SIDE, SIDE)
        spatial = lax.conv_general_dilated(maps, spatial_weight.astype(jnp.float32), (1, 1), 'SAME', dimension_numbers=('NCHW', 'OIHW', 'NCHW'), precision=lax.Precision.HIGHEST).reshape(IMG_DEV, MID, MAP_PIXEL_COUNT)
        second = jnp.maximum(normalize(spatial, spatial_gain, spatial_shift), 0.0).astype(jnp.bfloat16)
        expanded = jnp.einsum('om,bmp->bop', expand_weight.astype(jnp.float32), second.astype(jnp.float32), precision=lax.Precision.HIGHEST)
        return normalize(expanded, expand_gain, expand_shift).astype(jnp.bfloat16)
    third = lax.map(block_group, shuffled).reshape(IMAGES, C, MAP_PIXEL_COUNT)

    def restore_group(pair):
        section, indices = pair
        restored = jnp.take(third, indices, axis=0)
        output = jnp.maximum(restored.astype(jnp.float32) + section.astype(jnp.float32), 0.0).astype(jnp.bfloat16)
        return (output, lax.optimization_barrier(jnp.mean(output.astype(jnp.float32), axis=2)))
    features, pooled = lax.map(restore_group, (grouped, inverse.reshape(N_DP, IMG_DEV)))
    features = features.reshape(IMAGES, C, MAP_PIXEL_COUNT)
    pooled = pooled.reshape(IMAGES, C)
    embedded = jnp.dot(pooled, projection.astype(jnp.float32), precision=lax.Precision.HIGHEST)
    momentum_embeddings_out = (embedded * lax.rsqrt(lax.optimization_barrier(jnp.sum(embedded * embedded, axis=1, keepdims=True)) + 1e-06)).astype(jnp.bfloat16)
    unit_length_probes = (queries * lax.rsqrt(lax.optimization_barrier(jnp.sum(queries * queries, axis=1, keepdims=True)) + 1e-06)).astype(jnp.bfloat16)
    matched_similarity_scores = jnp.dot(unit_length_probes, momentum_embeddings_out.T, preferred_element_type=jnp.float32) / sharpness_divisor
    stored_similarity_scores = jnp.dot(unit_length_probes, dictionary_bank.T, preferred_element_type=jnp.float32) / sharpness_divisor
    queue_mass = lax.optimization_barrier(jnp.sum(jnp.exp(stored_similarity_scores), axis=1))
    loss = jnp.log(lax.optimization_barrier(jnp.sum(jnp.exp(matched_similarity_scores), axis=1)) + queue_mass) - jnp.diagonal(matched_similarity_scores)
    return (features, matched_similarity_scores, loss)
```

```python
import jax
import jax.numpy as jnp
from jax import lax
from jax.experimental import pallas as pl
from jax.experimental.pallas import tpu as pltpu
from jax.sharding import PartitionSpec as P

MESH = pl.DeviceIdType.MESH
F32 = jnp.float32
BF16 = jnp.bfloat16

SIDE = 56
PIXELS = SIDE * SIDE
COLS = 64
CHIPS = 64
ROWS = 16
QUARTER = PIXELS // 4 // 16
FULL = ROWS * SIDE // 16
HALF = FULL // 2
BACK = QUARTER + 1
A_TILES = 25
COUNT = 2.0 * (PIXELS // 4)
DIVISOR = 0.2


def nt(a, b):
    return lax.dot_general(a, b, (((1,), (1,)), ((), ())), preferred_element_type=F32)


def tn(a, b):
    return lax.dot_general(a, b, (((0,), (1,)), ((), ())), preferred_element_type=F32)


def remote(src, dst, send, recv, device):
    return pltpu.make_async_remote_copy(
        src_ref=src,
        dst_ref=dst,
        send_sem=send,
        recv_sem=recv,
        device_id=device,
        device_id_type=MESH,
    )


def bytes_of(ref, sem):
    pltpu.make_async_copy(ref, ref, sem).wait()


def kernel(
    perm,
    inv,
    img_hbm,
    rw,
    cw,
    we,
    vin,
    proj,
    queries,
    bank,
    feat,
    score_out,
    loss_out,
    img,
    part,
    from_left,
    from_right,
    via_left,
    via_right,
    sum_a,
    sum_b,
    conv_w,
    exp_w,
    vecs,
    field,
    hold1,
    out1,
    group,
    stat1,
    stat2,
    stat3s,
    stat3,
    mid,
    hold2,
    out2,
    home,
    second_all,
    emb,
    keys1,
    keys2,
    img_sem,
    rs_send,
    rs_recv,
    w_send,
    w_recv,
    s_send,
    s_recv,
    hop_send,
    hop_recv,
    pair_send,
    pair_recv,
    ag_send,
    ag_recv,
    e_send,
    e_recv,
    k_send,
    k_recv,
):
    dp = lax.axis_index("dp")
    mp = lax.axis_index("mp")
    me = dp // 2
    core = dp % 2
    other = dp + 1 - 2 * core
    right = (mp + 1) % 4
    left = (mp + 3) % 4
    far = (mp + 2) % 4

    fetch = pltpu.make_async_copy(img_hbm, img, img_sem)
    fetch.start()

    barrier = pltpu.get_barrier_semaphore()

    def greet(i, carry):
        for u in range(7):
            h = (me + 1 + 7 * i + u) % CHIPS
            pl.semaphore_signal(barrier, inc=1, device_id=(h * 2 + core, mp), device_id_type=MESH)
        return carry

    for j in range(1, 4):
        pl.semaphore_signal(barrier, inc=1, device_id=(dp, (mp + j) % 4), device_id_type=MESH)
    for j in range(4):
        pl.semaphore_signal(barrier, inc=1, device_id=(other, (mp + j) % 4), device_id_type=MESH)
    lax.fori_loop(0, 9, greet, 0)

    row128 = lax.broadcasted_iota(jnp.int32, (128, 384), 0) // 64
    lane128 = (lax.broadcasted_iota(jnp.int32, (128, 384), 1) // 64) % 2
    same = row128 == lane128
    eye_block = same[:, 0:128]

    def doubled(w):
        w = w.astype(F32)
        return jnp.concatenate([w, w], axis=1)

    def diagonal(w):
        return jnp.where(eye_block, jnp.concatenate([w, w], axis=0), 0.0).astype(BF16)

    rw_block = diagonal(doubled(rw[...]))
    we_wide = doubled(we[...])
    we_block = diagonal(we_wide)
    v_row = lax.broadcasted_iota(jnp.int32, (8, 192), 0)
    v_lane = lax.broadcasted_iota(jnp.int32, (8, 192), 1)
    v_in = jnp.where(v_lane // 16 == v_row, jnp.broadcast_to(vin[...], (8, 192)), 0.0)
    v_in = jnp.where(v_row < 4, v_in, 0.0)
    p_row = lax.broadcasted_iota(jnp.int32, (192, 128), 0)
    p_lane = lax.broadcasted_iota(jnp.int32, (192, 128), 1)
    v_place = jnp.where(p_row % 16 + 16 * mp == p_lane % 64, 1.0, 0.0)
    vec = jnp.dot(v_in, v_place, precision=lax.Precision.HIGHEST, preferred_element_type=F32)
    c_row = lax.broadcasted_iota(jnp.int32, (128, 192), 0) % 64
    c_lane = lax.broadcasted_iota(jnp.int32, (128, 192), 1)
    v_all = jnp.broadcast_to(vin[...], (128, 192))
    gain_c = jnp.sum(jnp.where(c_lane == c_row + 64, v_all, 0.0), axis=1, keepdims=True)
    shift_c = jnp.sum(jnp.where(c_lane == c_row + 128, v_all, 0.0), axis=1, keepdims=True)
    fetch.wait()

    part[0:3] = jnp.zeros((3, 16, 128), BF16)
    tail = jnp.zeros((8, 128), F32)
    for k in range(5):
        wide = 640 if k < 4 else 576
        block = tn(img[:, 640 * k : 640 * k + wide], rw_block)
        if k < 4:
            rows = jnp.concatenate([tail, block[:632]], axis=0)
            tail = block[632:640]
        else:
            rows = jnp.concatenate([tail, block, jnp.zeros((56, 128), F32)], axis=0)
        part[40 * k + 3 : 40 * k + 43] = rows.astype(BF16).reshape(40, 16, 128)

    conv_w[mp] = cw[...]
    exp_w[mp] = we_wide.astype(BF16)
    vecs[mp] = vec

    pl.semaphore_wait(barrier, CHIPS - 1 + 7)

    def tiles(q, start, n):
        return part.at[pl.ds(QUARTER * q + start, n)]

    to_r = (dp, right)
    to_l = (dp, left)
    rs = [
        remote(tiles(far, 0, HALF), via_left, rs_send.at[0], rs_recv.at[0], to_r),
        remote(tiles(far, HALF, HALF), via_right, rs_send.at[1], rs_recv.at[1], to_l),
        remote(tiles(right, HALF, HALF), from_left.at[pl.ds(HALF, HALF)], rs_send.at[2], rs_recv.at[2], to_r),
        remote(tiles(left, 0, HALF), from_right.at[pl.ds(0, HALF)], rs_send.at[3], rs_recv.at[3], to_l),
        remote(sum_a, from_left.at[pl.ds(0, HALF)], rs_send.at[4], rs_recv.at[4], to_r),
        remote(sum_b, from_right.at[pl.ds(HALF, HALF)], rs_send.at[5], rs_recv.at[5], to_l),
    ]
    for copy in rs[:4]:
        copy.start()

    def share(buf, n):
        copies = [
            remote(buf.at[mp], buf.at[mp], w_send.at[n, j - 1], w_recv.at[n, j - 1], (dp, (mp + j) % 4))
            for j in range(1, 4)
        ]
        for copy in copies:
            copy.start()
        return copies

    def shared(buf, copies, n):
        for j in range(1, 4):
            src = buf.at[(mp + 4 - j) % 4]
            bytes_of(src, w_recv.at[n, j - 1])

    sent = []

    q_row = lax.broadcasted_iota(jnp.int32, (16, 128), 0)
    q_all = jnp.where(q_row == 0, queries[0:1, :], jnp.where(q_row == 1, queries[1:2, :], 0.0))
    unit = (q_all * lax.rsqrt(jnp.sum(q_all * q_all, axis=1, keepdims=True) + 1e-06)).astype(BF16)
    stored = nt(unit, bank[...]) / DIVISOR
    mass = jnp.broadcast_to(jnp.sum(jnp.exp(stored), axis=1, keepdims=True), (16, 128))

    rs[0].wait_recv()
    own = part[pl.ds(QUARTER * right, HALF)].astype(F32)
    sum_a[...] = (own + via_left[...].astype(F32)).astype(BF16)
    rs[4].start()
    rs[1].wait_recv()
    own = part[pl.ds(QUARTER * left + HALF, HALF)].astype(F32)
    sum_b[...] = (own + via_right[...].astype(F32)).astype(BF16)
    rs[5].start()

    sent += share(conv_w, 0)
    sent += share(exp_w, 1)
    sent += share(vecs, 2)

    for copy in rs[2:]:
        copy.wait_recv()
    total = (
        part[pl.ds(QUARTER * mp, FULL)].astype(F32)
        + from_left[...].astype(F32)
        + from_right[...].astype(F32)
    )
    total = total.reshape(ROWS, SIDE, 128)
    total = jnp.concatenate([total, jnp.zeros((ROWS, COLS - SIDE, 128), F32)], axis=1)
    field[...] = total.reshape(CHIPS, 16, 128).astype(BF16)

    low = lax.broadcasted_iota(jnp.int32, (16, 128), 1) < 64

    def send_tile(src, hold, h, slot):
        remote(
            src.at[h], hold.at[me, core, 0], hop_send.at[slot], hop_recv.at[slot], (h * 2 + core, mp)
        ).start()

    def spread(src, hold, late, n, slot):
        def step(i, carry):
            for u in range(7):
                h = (me + 1 + 7 * i + u) % CHIPS

                @pl.when(jnp.logical_and(h != late, h < n))
                def _():
                    send_tile(src, hold, h, slot)

            return carry

        lax.fori_loop(0, 9, step, 0)

        @pl.when(jnp.logical_and(me != late, me < n))
        def _():
            hold[me, core, 0] = src[me]

    def spread_late(src, hold, late, slot):
        @pl.when(me != late)
        def _():
            send_tile(src, hold, late, slot)

        @pl.when(me == late)
        def _():
            hold[late, core, 0] = src[late]

    def permute(hold, order, out, dst, n, slot):
        def turn(side):
            x = hold[:, side, 0].reshape(CHIPS * 16, 128).astype(F32)
            hold[:, side, 1] = pltpu.roll(x, 64, 1).astype(BF16).reshape(CHIPS, 16, 128)

        def pick(t):
            at = 4 * t + 2 * core
            i0 = order[at]
            i1 = order[at + 1]
            x0 = hold[i0 >> 2, (i0 >> 1) & 1, i0 & 1]
            x1 = hold[i1 >> 2, (i1 >> 1) & 1, 1 - (i1 & 1)]
            return jnp.where(low, x0, x1)

        @pl.when(me < n)
        def _():
            bytes_of(hold.at[pl.ds(0, CHIPS - 1), core, 0], hop_recv.at[slot])
            swap = remote(
                hold.at[:, core, 0], hold.at[:, core, 0], pair_send.at[slot], pair_recv.at[slot], (other, mp)
            )
            swap.start()
            turn(core)
            bytes_of(hold.at[:, 1 - core, 0], pair_recv.at[slot])
            turn(1 - core)

            def step(i, carry):
                ts = [(me + 1 + 9 * i + u) % CHIPS for u in range(9)]
                values = [pick(t) for t in ts]
                for t, value in zip(ts, values):
                    out[t] = value
                for t in ts:
                    remote(
                        out.at[t],
                        dst.at[me],
                        hop_send.at[slot + 1],
                        hop_recv.at[slot + 1],
                        (t * 2 + core, mp),
                    ).start()
                return carry

            lax.fori_loop(0, 7, step, 0)
            dst[me] = pick(me)
            swap.wait_send()
            bytes_of(dst.at[pl.ds(0, n - 1)], hop_recv.at[slot + 1])

        if n < CHIPS:

            @pl.when(me >= n)
            def _():
                bytes_of(dst, hop_recv.at[slot + 1])

    def both(x):
        x = jnp.broadcast_to(x, (8, 128))
        return x + pltpu.roll(x, 64, 1)

    def offer(buf, tile, n):
        buf[mp] = tile
        copies = [
            remote(buf.at[mp], buf.at[mp], s_send.at[n, j - 1], s_recv.at[n, j - 1], (dp, (mp + j) % 4))
            for j in range(1, 4)
        ]
        for copy in copies:
            copy.start()
        return copies

    def collect(buf, n):
        for j in range(1, 4):
            bytes_of(buf.at[(mp + 4 - j) % 4], s_recv.at[n, j - 1])

    def local_stats(x):
        mean = both(jnp.sum(x, axis=0, keepdims=True)) / COUNT
        dev = x - mean[0:1]
        square = both(jnp.sum(dev * dev, axis=0, keepdims=True))
        return jnp.concatenate([mean, square], axis=0)

    def whole_stats(buf, count):
        means = [buf[q, 0:1, :] for q in range(4)]
        mean = (means[0] + means[1] + means[2] + means[3]) * 0.25
        square = jnp.zeros((1, 128), F32)
        for q in range(4):
            off = means[q] - mean
            square = square + buf[q, 8:9, :] + count * (off * off)
        return mean, square / (4.0 * count)

    def pieces(v):
        a = v.astype(BF16).astype(F32)
        b = (v - a).astype(BF16).astype(F32)
        return [a, b, v - a - b]

    spread(field, hold1, 3, CHIPS, 0)
    x = field[...].reshape(ROWS * COLS, 128).astype(F32)
    at = lax.broadcasted_iota(jnp.int32, (ROWS * COLS, 128), 0)
    line = at // COLS
    column = at % COLS
    inner = jnp.logical_and(jnp.logical_and(line >= 1, line <= ROWS - 2), column < SIDE)
    half_count = COUNT / 2.0
    mean = jnp.sum(jnp.where(inner, x, 0.0), axis=0, keepdims=True) / half_count
    dev = jnp.where(inner, x - mean, 0.0)
    square = jnp.sum(dev * dev, axis=0, keepdims=True)
    tile = jnp.concatenate([jnp.broadcast_to(mean, (8, 128)), jnp.broadcast_to(square, (8, 128))], axis=0)
    sent_stats = offer(stat1, tile, 0)
    collect(stat1, 0)
    mean, var = whole_stats(stat1, half_count)
    tile = field[3].astype(F32)
    for r, v in enumerate(pieces(mean) + pieces(var)):
        tile = jnp.where(q_row == 8 + r, v, tile)
    field[3] = tile.astype(BF16)
    spread_late(field, hold1, 3, 0)

    for n, buf in enumerate((conv_w, exp_w, vecs)):
        shared(buf, sent, n)
    conv_blocks = []
    for dy in range(3):
        w = jnp.concatenate([conv_w[q, dy] for q in range(4)] * 2, axis=0).astype(F32)
        conv_blocks.append(jnp.where(same, w, 0.0).astype(BF16))
    vec_all = vecs[0] + vecs[1] + vecs[2] + vecs[3]
    permute(hold1, perm, out1, group, CHIPS, 0)


    marks = group[3].astype(F32)
    mean_i = marks[8:9] + marks[9:10] + marks[10:11]
    var_i = marks[11:12] + marks[12:13] + marks[13:14]
    mean = (both(mean_i) * 0.5)[0:1]
    off = mean_i - mean
    var = (both(var_i + off * off) * 0.5)[0:1]
    x = group[...].reshape(ROWS * COLS, 128).astype(F32)
    true_line = line + (ROWS - 2) * mp - 1
    inside = jnp.logical_and(jnp.logical_and(true_line >= 0, true_line < SIDE), column < SIDE)
    first = jnp.maximum((x - mean) * lax.rsqrt(var + 1e-05) * vec_all[0:1] + vec_all[1:2], 0.0)
    first = jnp.where(inside, first, 0.0)

    wide = jnp.concatenate(
        [
            pltpu.roll(first, 1, 0).astype(BF16),
            first.astype(BF16),
            pltpu.roll(first, ROWS * COLS - 1, 0).astype(BF16),
        ],
        axis=1,
    )
    n_out = (ROWS - 2) * COLS
    spatial = nt(wide[0:n_out], conv_blocks[0])
    spatial = spatial + nt(wide[COLS : COLS + n_out], conv_blocks[1])
    spatial = spatial + nt(wide[2 * COLS : 2 * COLS + n_out], conv_blocks[2])
    spatial = spatial.reshape(ROWS - 2, COLS, 128)[:, :SIDE, :].reshape(16 * QUARTER, 128)

    sent_stats += offer(stat2, local_stats(spatial), 1)
    collect(stat2, 1)
    mean, var = whole_stats(stat2, COUNT)
    second = jnp.maximum((spatial - mean) * lax.rsqrt(var + 1e-05) * vec_all[2:3] + vec_all[3:4], 0.0).astype(BF16)
    mid[0:QUARTER] = second.reshape(QUARTER, 16, 128)
    spread(mid, hold2, QUARTER, QUARTER, 2)

    copies3 = []
    for q in range(4):
        stat3s[q] = local_stats(nt(second, diagonal(exp_w[q].astype(F32))))
    for j in range(1, 4):
        q = (mp + j) % 4
        copy = remote(stat3s.at[q], stat3.at[mp], s_send.at[2, j - 1], s_recv.at[2, j - 1], (dp, q))
        copy.start()
        copies3.append(copy)
    stat3[mp] = stat3s[mp]
    collect(stat3, 2)
    sent_stats += copies3
    mean, var = whole_stats(stat3, COUNT)
    scale = lax.rsqrt(var + 1e-05)
    tile = jnp.zeros((16, 128), F32)
    for r, v in enumerate(pieces(mean) + pieces(scale)):
        tile = jnp.where(q_row == r, v, tile)
    mid[QUARTER] = tile.astype(BF16)
    spread_late(mid, hold2, QUARTER, 2)
    permute(hold2, inv, out2, home, BACK, 2)

    second_all[pl.ds(QUARTER * mp, QUARTER)] = home[0:QUARTER]
    b_tiles = QUARTER - A_TILES

    def a_of(q):
        return second_all.at[pl.ds(QUARTER * q, A_TILES)]

    def b_of(q):
        return second_all.at[pl.ds(QUARTER * q + A_TILES, b_tiles)]

    ag = [
        remote(a_of(mp), a_of(mp), ag_send.at[0], ag_recv.at[0], to_r),
        remote(b_of(mp), b_of(mp), ag_send.at[1], ag_recv.at[1], to_l),
        remote(b_of(mp), b_of(mp), ag_send.at[2], ag_recv.at[2], to_r),
        remote(a_of(mp), a_of(mp), ag_send.at[3], ag_recv.at[3], to_l),
        remote(a_of(left), a_of(left), ag_send.at[4], ag_recv.at[4], to_r),
        remote(b_of(right), b_of(right), ag_send.at[5], ag_recv.at[5], to_l),
    ]
    for copy in ag[:4]:
        copy.start()
    bytes_of(a_of(left), ag_recv.at[0])
    ag[4].start()
    bytes_of(b_of(right), ag_recv.at[1])
    ag[5].start()

    identity = jnp.where(
        lax.broadcasted_iota(jnp.int32, (128, 128), 0) == lax.broadcasted_iota(jnp.int32, (128, 128), 1),
        1.0,
        0.0,
    ).astype(BF16)
    columns = nt(identity, home[QUARTER])
    mean_c = columns[:, 0:1] + columns[:, 1:2] + columns[:, 2:3]
    scale_c = columns[:, 3:4] + columns[:, 4:5] + columns[:, 5:6]

    bytes_of(b_of(left), ag_recv.at[2])
    bytes_of(a_of(right), ag_recv.at[3])
    bytes_of(a_of(far), ag_recv.at[4])
    bytes_of(b_of(far), ag_recv.at[5])

    pooled = jnp.zeros((128, 1), F32)
    for k in range(5):
        n = 40 if k < 4 else 36
        block = second_all[40 * k : 40 * k + n].reshape(16 * n, 128)
        v = nt(we_block, block)
        third = ((v - mean_c) * scale_c * gain_c + shift_c).astype(BF16).astype(F32)
        lanes = slice(640 * k, 640 * k + 16 * n)
        f = jnp.maximum(third + img[:, lanes].astype(F32), 0.0).astype(BF16)
        feat[:, lanes] = f
        pooled = pooled + jnp.sum(f.astype(F32), axis=1, keepdims=True)
    pooled = pooled / float(PIXELS)

    proj2 = jnp.concatenate([proj[...], proj[...]], axis=0).astype(F32)
    terms = pooled * proj2
    e0 = jnp.sum(terms[0:64], axis=0, keepdims=True)
    e1 = jnp.sum(terms[64:128], axis=0, keepdims=True)
    row8 = lax.broadcasted_iota(jnp.int32, (8, 128), 0)
    top = jnp.where(row8 == 0, e0, jnp.where(row8 == 1, e1, 0.0))
    emb[core, mp] = jnp.concatenate([top, mass[0:8]], axis=0)
    mine = emb.at[core, mp]
    e_copies = []
    for j in range(1, 4):
        e_copies.append(remote(mine, mine, e_send.at[j], e_recv.at[j], (dp, (mp + j) % 4)))
    for j in range(4):
        e_copies.append(remote(mine, mine, e_send.at[4 + j], e_recv.at[4 + j], (other, (mp + j) % 4)))
    for copy in e_copies:
        copy.start()
    for j in range(1, 4):
        bytes_of(emb.at[core, (mp + 4 - j) % 4], e_recv.at[j])
    for j in range(4):
        bytes_of(emb.at[1 - core, (mp + 4 - j) % 4], e_recv.at[4 + j])

    key_tile = jnp.zeros((16, 128), F32)
    for cc in range(2):
        e = emb[cc, 0, 0:8] + emb[cc, 1, 0:8] + emb[cc, 2, 0:8] + emb[cc, 3, 0:8]
        key = e * lax.rsqrt(jnp.sum(e * e, axis=1, keepdims=True) + 1e-06)
        for b in range(2):
            here = q_row == 4 * (me % 4) + 2 * cc + b
            key_tile = jnp.where(here, key[b : b + 1], key_tile)
    queue = emb[core, 0, 8:16] + emb[core, 1, 8:16] + emb[core, 2, 8:16] + emb[core, 3, 8:16]
    z = me % 8
    slab = me // 8
    keys1[z] = key_tile.astype(BF16)
    k_copies = []
    for j in range(1, 8):
        h = slab * 8 + (z + j) % 8
        k_copies.append(remote(keys1.at[z], keys1.at[z], k_send.at[0, j], k_recv.at[0, j], (h * 2 + core, mp)))
    for copy in k_copies:
        copy.start()
    for j in range(1, 8):
        bytes_of(keys1.at[(z + 8 - j) % 8], k_recv.at[0, j])
    keys2[slab] = jnp.sum(keys1[...].astype(F32).reshape(2, 4, 16, 128), axis=1).astype(BF16)
    k_copies2 = []
    for j in range(1, 8):
        h = (me + 8 * j) % CHIPS
        k_copies2.append(
            remote(keys2.at[slab], keys2.at[slab], k_send.at[1, j], k_recv.at[1, j], (h * 2 + core, mp))
        )
    for copy in k_copies2:
        copy.start()
    for j in range(1, 8):
        bytes_of(keys2.at[(slab + 8 - j) % 8], k_recv.at[1, j])
    every = keys2[...].reshape(256, 128)
    score = (nt(unit, every) / DIVISOR)[0:8]
    score_out[...] = score[0:2]
    lane = lax.broadcasted_iota(jnp.int32, (8, 256), 1)
    row = lax.broadcasted_iota(jnp.int32, (8, 256), 0)
    matched = jnp.sum(jnp.where(lane == 2 * dp + row, score, 0.0), axis=1, keepdims=True)
    mass_all = jnp.sum(jnp.exp(score), axis=1, keepdims=True) + queue[:, 0:1]
    losses = jnp.broadcast_to(jnp.log(mass_all) - matched, (8, 128))
    lane8 = lax.broadcasted_iota(jnp.int32, (8, 128), 1)
    loss_out[...] = jnp.sum(jnp.where(row8 == lane8, losses, 0.0), axis=0, keepdims=True)[:, 0:2]

    for copy in rs + sent + sent_stats + ag + e_copies + k_copies + k_copies2:
        copy.wait_send()
    bytes_of(field.at[pl.ds(0, CHIPS - 1)], hop_send.at[0])
    bytes_of(out1.at[pl.ds(0, CHIPS - 1)], hop_send.at[1])

    @pl.when(me < BACK)
    def _():
        bytes_of(mid.at[pl.ds(0, BACK - 1)], hop_send.at[2])
        bytes_of(out2.at[pl.ds(0, CHIPS - 1)], hop_send.at[3])

    @pl.when(me >= BACK)
    def _():
        bytes_of(mid, hop_send.at[2])


def on_device(
    images,
    permutation,
    inverse,
    reduce_weight,
    reduce_gain,
    reduce_shift,
    spatial_weight,
    spatial_gain,
    spatial_shift,
    expand_weight,
    expand_gain,
    expand_shift,
    projection,
    queries,
    dictionary_bank,
):
    cw = jnp.transpose(spatial_weight, (2, 0, 3, 1))
    cw = jnp.stack([cw, cw], axis=3).reshape(3, 16, 384)
    vin = jnp.concatenate(
        [reduce_gain, reduce_shift, spatial_gain, spatial_shift, expand_gain, expand_shift]
    ).reshape(1, 192)

    vmem = pl.BlockSpec(memory_space=pltpu.VMEM)
    smem = pl.BlockSpec(memory_space=pltpu.SMEM)
    dma = pltpu.SemaphoreType.DMA
    feat, score, loss = pl.pallas_call(
        kernel,
        out_shape=(
            jax.ShapeDtypeStruct((128, PIXELS), BF16),
            jax.ShapeDtypeStruct((2, 256), F32),
            jax.ShapeDtypeStruct((1, 2), F32),
        ),
        in_specs=[smem, smem, pl.BlockSpec(memory_space=pl.ANY)] + [vmem] * 7,
        out_specs=(vmem, vmem, vmem),
        scratch_shapes=[
            pltpu.VMEM((128, PIXELS), BF16),
            pltpu.VMEM((203, 16, 128), BF16),
            pltpu.VMEM((FULL, 16, 128), BF16),
            pltpu.VMEM((FULL, 16, 128), BF16),
            pltpu.VMEM((HALF, 16, 128), BF16),
            pltpu.VMEM((HALF, 16, 128), BF16),
            pltpu.VMEM((HALF, 16, 128), BF16),
            pltpu.VMEM((HALF, 16, 128), BF16),
            pltpu.VMEM((4, 3, 16, 384), BF16),
            pltpu.VMEM((4, 64, 128), BF16),
            pltpu.VMEM((4, 8, 128), F32),
            pltpu.VMEM((CHIPS, 16, 128), BF16),
            pltpu.VMEM((CHIPS, 2, 2, 16, 128), BF16),
            pltpu.VMEM((CHIPS, 16, 128), BF16),
            pltpu.VMEM((CHIPS, 16, 128), BF16),
            pltpu.VMEM((4, 16, 128), F32),
            pltpu.VMEM((4, 16, 128), F32),
            pltpu.VMEM((4, 16, 128), F32),
            pltpu.VMEM((4, 16, 128), F32),
            pltpu.VMEM((BACK, 16, 128), BF16),
            pltpu.VMEM((CHIPS, 2, 2, 16, 128), BF16),
            pltpu.VMEM((CHIPS, 16, 128), BF16),
            pltpu.VMEM((BACK, 16, 128), BF16),
            pltpu.VMEM((4 * QUARTER, 16, 128), BF16),
            pltpu.VMEM((2, 4, 16, 128), F32),
            pltpu.VMEM((8, 16, 128), BF16),
            pltpu.VMEM((8, 2, 16, 128), BF16),
            dma,
            dma((6,)),
            dma((6,)),
            dma((3, 3)),
            dma((3, 3)),
            dma((3, 3)),
            dma((3, 3)),
            dma((4,)),
            dma((4,)),
            dma((4,)),
            dma((4,)),
            dma((6,)),
            dma((6,)),
            dma((8,)),
            dma((8,)),
            dma((2, 8)),
            dma((2, 8)),
        ],
        compiler_params=pltpu.CompilerParams(
            collective_id=0, has_side_effects=True, vmem_limit_bytes=48 * 1024 * 1024
        ),
        cost_estimate=pl.CostEstimate(
            flops=2 * 3136 * 128 * 128 * 4, bytes_accessed=2 * 128 * 3136 * 2, transcendentals=0
        ),
    )(
        permutation,
        inverse,
        images.reshape(128, PIXELS),
        reduce_weight,
        cw,
        expand_weight,
        vin,
        projection,
        queries,
        dictionary_bank,
    )
    return feat.reshape(images.shape), score, loss.reshape(2)


def solution(mesh):
    placed = (
        P("dp", "mp", None),
        P(),
        P(),
        P(None, "mp"),
        P("mp"),
        P("mp"),
        P("mp", None, None, None),
        P("mp"),
        P("mp"),
        P("mp", None),
        P("mp"),
        P("mp"),
        P("mp", None),
        P("dp", None),
        P("mp", None),
    )
    return jax.shard_map(
        on_device,
        mesh=mesh,
        in_specs=placed,
        out_specs=(P("dp", "mp", None), P("dp", None), P("dp")),
        check_vma=False,
    )
```

```python
import jax
import jax.numpy as jnp
from jax import lax
from jax.experimental import pallas as pl
from jax.experimental.pallas import tpu as pltpu
from jax.sharding import PartitionSpec as P

MESH = pl.DeviceIdType.MESH
F32 = jnp.float32
BF16 = jnp.bfloat16

SIDE = 56
PIXELS = SIDE * SIDE
COLS = 64
CHIPS = 64
LINES = SIDE // 4
QUARTER = PIXELS // 4 // 16
A_TILES = 25
B_TILES = QUARTER - A_TILES
BACK = QUARTER + 1
STAT_CHIP = CHIPS - 1
COUNT = 2.0 * (PIXELS // 4)
DIVISOR = 0.2


def nt(a, b):
    return lax.dot_general(a, b, (((1,), (1,)), ((), ())), preferred_element_type=F32)


def tn(a, b):
    return lax.dot_general(a, b, (((0,), (1,)), ((), ())), preferred_element_type=F32)


def remote(src, dst, send, recv, device):
    return pltpu.make_async_remote_copy(
        src_ref=src,
        dst_ref=dst,
        send_sem=send,
        recv_sem=recv,
        device_id=device,
        device_id_type=MESH,
    )


def bytes_of(ref, sem):
    pltpu.make_async_copy(ref, ref, sem).wait()


def kernel(
    perm,
    inv,
    img_hbm,
    rw,
    cw,
    we,
    rg,
    rsh,
    sg,
    ssh,
    eg,
    esh,
    proj,
    queries,
    bank,
    feat_hbm,
    score_out,
    loss_out,
    img,
    feat,
    part,
    from_left,
    from_right,
    via_left,
    via_right,
    sum_a,
    sum_b,
    conv_w,
    exp_w,
    vecs,
    field,
    hold1,
    out1,
    group,
    stat1,
    stat2,
    stat3s,
    stat3,
    mid,
    hold2,
    out2,
    home,
    second_all,
    emb,
    keys1,
    keys2,
    halo_top,
    halo_bottom,
    img_sem,
    feat_sem,
    rs_send,
    rs_recv,
    w_send,
    w_recv,
    s_send,
    s_recv,
    hop_send,
    hop_recv,
    out_send,
    out_recv,
    halo_send,
    halo_recv,
    pair_send,
    pair_recv,
    ag_send,
    ag_recv,
    e_send,
    e_recv,
    k_send,
    k_recv,
):
    dp = lax.axis_index("dp")
    mp = lax.axis_index("mp")
    me = dp // 2
    core = dp % 2
    other = dp + 1 - 2 * core
    right = (mp + 1) % 4
    left = (mp + 3) % 4
    far = (mp + 2) % 4

    fetch = pltpu.make_async_copy(img_hbm, img, img_sem)
    fetch.start()

    barrier = pltpu.get_barrier_semaphore()

    def greet(i, carry):
        for u in range(7):
            h = (me + 1 + 7 * i + u) % CHIPS
            pl.semaphore_signal(barrier, inc=1, device_id=(h * 2 + core, mp), device_id_type=MESH)
        return carry

    for j in range(1, 4):
        pl.semaphore_signal(barrier, inc=1, device_id=(dp, (mp + j) % 4), device_id_type=MESH)
    for j in range(4):
        pl.semaphore_signal(barrier, inc=1, device_id=(other, (mp + j) % 4), device_id_type=MESH)
    lax.fori_loop(0, 9, greet, 0)

    row128 = lax.broadcasted_iota(jnp.int32, (128, 384), 0) // 64
    lane128 = (lax.broadcasted_iota(jnp.int32, (128, 384), 1) // 64) % 2
    same = row128 == lane128
    eye_block = same[:, 0:128]

    def doubled(w):
        w = w.astype(F32)
        return jnp.concatenate([w, w], axis=1)

    def diagonal(w):
        return jnp.where(eye_block, jnp.concatenate([w, w], axis=0), 0.0).astype(BF16)

    rw_block = diagonal(doubled(rw[...]))
    fetch.wait()

    for k in range(5):
        n = 40 if k < 4 else 36
        block = tn(img[:, 640 * k : 640 * k + 16 * n], rw_block)
        part[40 * k : 40 * k + n] = block.astype(BF16).reshape(n, 16, 128)

    pl.semaphore_wait(barrier, CHIPS - 1 + 7)

    def a_part(q):
        return part.at[pl.ds(QUARTER * q, A_TILES)]

    def b_part(q):
        return part.at[pl.ds(QUARTER * q + A_TILES, B_TILES)]

    to_r = (dp, right)
    to_l = (dp, left)
    left_a = from_left.at[pl.ds(0, A_TILES)]
    left_b = from_left.at[pl.ds(A_TILES, B_TILES)]
    right_a = from_right.at[pl.ds(0, A_TILES)]
    right_b = from_right.at[pl.ds(A_TILES, B_TILES)]
    rs = [
        remote(a_part(far), via_left, rs_send.at[0], rs_recv.at[0], to_r),
        remote(a_part(left), right_a, rs_send.at[1], rs_recv.at[1], to_l),
        remote(b_part(right), left_b, rs_send.at[2], rs_recv.at[2], to_r),
        remote(b_part(far), via_right, rs_send.at[3], rs_recv.at[3], to_l),
        remote(sum_a, left_a, rs_send.at[4], rs_recv.at[4], to_r),
        remote(sum_b, right_b, rs_send.at[5], rs_recv.at[5], to_l),
    ]
    for copy in rs[:4]:
        copy.start()

    vin = jnp.concatenate([rg[...], rsh[...], sg[...], ssh[...], eg[...], esh[...]], axis=1)
    we_wide = doubled(we[...])
    we_block = diagonal(we_wide)
    v_row = lax.broadcasted_iota(jnp.int32, (8, 192), 0)
    v_lane = lax.broadcasted_iota(jnp.int32, (8, 192), 1)
    v_in = jnp.where(v_lane // 16 == v_row, jnp.broadcast_to(vin, (8, 192)), 0.0)
    v_in = jnp.where(v_row < 4, v_in, 0.0)
    p_row = lax.broadcasted_iota(jnp.int32, (192, 128), 0)
    p_lane = lax.broadcasted_iota(jnp.int32, (192, 128), 1)
    v_place = jnp.where(p_row % 16 + 16 * mp == p_lane % 64, 1.0, 0.0)
    vec = jnp.dot(v_in, v_place, precision=lax.Precision.HIGHEST, preferred_element_type=F32)
    c_row = lax.broadcasted_iota(jnp.int32, (128, 192), 0) % 64
    c_lane = lax.broadcasted_iota(jnp.int32, (128, 192), 1)
    v_all = jnp.broadcast_to(vin, (128, 192))
    gain_c = jnp.sum(jnp.where(c_lane == c_row + 64, v_all, 0.0), axis=1, keepdims=True)
    shift_c = jnp.sum(jnp.where(c_lane == c_row + 128, v_all, 0.0), axis=1, keepdims=True)
    for dy in range(3):
        conv_w[mp, dy] = jnp.concatenate([doubled(cw[dy, dx]) for dx in range(3)], axis=1).astype(BF16)
    exp_w[mp] = we_wide.astype(BF16)
    vecs[mp] = vec

    def share(buf, n):
        copies = [
            remote(buf.at[mp], buf.at[mp], w_send.at[n, j - 1], w_recv.at[n, j - 1], (dp, (mp + j) % 4))
            for j in range(1, 4)
        ]
        for copy in copies:
            copy.start()
        return copies

    def shared(buf, copies, n):
        for j in range(1, 4):
            src = buf.at[(mp + 4 - j) % 4]
            bytes_of(src, w_recv.at[n, j - 1])

    sent = []

    q_row = lax.broadcasted_iota(jnp.int32, (16, 128), 0)
    q_all = jnp.where(q_row == 0, queries[0:1, :], jnp.where(q_row == 1, queries[1:2, :], 0.0))
    unit = (q_all * lax.rsqrt(jnp.sum(q_all * q_all, axis=1, keepdims=True) + 1e-06)).astype(BF16)
    stored = nt(unit, bank[...]) / DIVISOR
    mass = jnp.broadcast_to(jnp.sum(jnp.exp(stored), axis=1, keepdims=True), (16, 128))

    rs[0].wait_recv()
    own = part[pl.ds(QUARTER * right, A_TILES)].astype(F32)
    sum_a[...] = (own + via_left[...].astype(F32)).astype(BF16)
    rs[4].start()
    rs[3].wait_recv()
    own = part[pl.ds(QUARTER * left + A_TILES, B_TILES)].astype(F32)
    sum_b[...] = (own + via_right[...].astype(F32)).astype(BF16)
    rs[5].start()

    sent += share(conv_w, 0)
    sent += share(exp_w, 1)
    sent += share(vecs, 2)

    low = lax.broadcasted_iota(jnp.int32, (16, 128), 1) < 64
    pair = me // 2
    holds_a = jnp.logical_and(me % 2 == 0, pair < A_TILES)
    holds_b = jnp.logical_and(me % 2 == 1, pair < B_TILES)
    holds_s = me == STAT_CHIP

    def send_tile(src, t, hold, h, slot):
        remote(
            src.at[t],
            hold.at[me, core, 0],
            hop_send.at[slot],
            hop_recv.at[slot, me // 8],
            (h * 2 + core, mp),
        ).start()

    def spread(src, hold, odd, slot):
        n = B_TILES if odd else A_TILES

        def step(i, carry):
            for u in range(8):
                t = (pair + 8 * i + u) % (CHIPS // 2)
                h = 2 * t + odd

                @pl.when(jnp.logical_and(h != me, t < n))
                def _():
                    send_tile(src, t + odd * A_TILES, hold, h, slot)

            return carry

        lax.fori_loop(0, 4, step, 0)

        @pl.when(holds_b if odd else holds_a)
        def _():
            hold[me, core, 0] = src[pair + odd * A_TILES]

    def spread_stats(src, hold, slot):
        @pl.when(me != STAT_CHIP)
        def _():
            send_tile(src, QUARTER, hold, STAT_CHIP, slot)

        @pl.when(holds_s)
        def _():
            hold[STAT_CHIP, core, 0] = src[QUARTER]

    def permute(hold, order, out, dst, slot, holds, tile, part_of):
        def turn(side, g):
            at = pl.ds(8 * g, 8)
            x = hold[at, side, 0].reshape(128, 128).astype(F32)
            hold[at, side, 1] = pltpu.roll(x, 64, 1).astype(BF16).reshape(8, 16, 128)

        def swapping(g):
            ref = hold.at[pl.ds(8 * g, 8), core, 0]
            return remote(ref, ref, pair_send.at[slot, g], pair_recv.at[slot, g], (other, mp))

        def take(i, carry):
            g = (me // 8 + 8 - i) % 8
            bytes_of(hold.at[pl.ds(8 * g, 8), core, 0], hop_recv.at[slot, g])
            swapping(g).start()
            turn(core, g)
            return carry

        def take_other(i, carry):
            g = (me // 8 + 8 - i) % 8
            bytes_of(hold.at[pl.ds(8 * g, 8), 1 - core, 0], pair_recv.at[slot, g])
            turn(1 - core, g)
            return carry

        def swapped(i, carry):
            swapping(i).wait_send()
            return carry

        def pick(t):
            at = 4 * t + 2 * core
            i0 = order[at]
            i1 = order[at + 1]
            x0 = hold[i0 >> 2, (i0 >> 1) & 1, i0 & 1]
            x1 = hold[i1 >> 2, (i1 >> 1) & 1, 1 - (i1 & 1)]
            return jnp.where(low, x0, x1)

        @pl.when(holds)
        def _():
            g = me // 8
            bytes_of(hold.at[pl.ds(8 * g, 7), core, 0], hop_recv.at[slot, g])
            swapping(g).start()
            turn(core, g)
            lax.fori_loop(1, 8, take, 0)
            lax.fori_loop(0, 8, take_other, 0)

            def step(i, carry):
                ts = [(me + 1 + 9 * i + u) % CHIPS for u in range(9)]
                values = [pick(t) for t in ts]
                for t, value in zip(ts, values):
                    out[t] = value
                for t in ts:
                    remote(
                        out.at[t],
                        dst.at[tile],
                        out_send.at[slot],
                        out_recv.at[slot, part_of],
                        (t * 2 + core, mp),
                    ).start()
                return carry

            lax.fori_loop(0, 7, step, 0)
            dst[tile] = pick(me)
            lax.fori_loop(0, 8, swapped, 0)

    def arrived(dst, slot, part_of):
        start, n, holds = ((0, A_TILES, holds_a), (A_TILES, B_TILES, holds_b), (QUARTER, 1, holds_s))[part_of]

        @pl.when(jnp.logical_not(holds))
        def _():
            bytes_of(dst.at[pl.ds(start, n)], out_recv.at[slot, part_of])

        if n > 1:

            @pl.when(holds)
            def _():
                bytes_of(dst.at[pl.ds(start, n - 1)], out_recv.at[slot, part_of])

    rs[4].wait_recv()
    rs[1].wait_recv()
    total = part[pl.ds(QUARTER * mp, A_TILES)].astype(F32)
    total = total + left_a[...].astype(F32) + right_a[...].astype(F32)
    field[0:A_TILES] = total.astype(BF16)
    spread(field, hold1, 0, 0)

    rs[2].wait_recv()
    rs[5].wait_recv()
    total = part[pl.ds(QUARTER * mp + A_TILES, B_TILES)].astype(F32)
    total = total + left_b[...].astype(F32) + right_b[...].astype(F32)
    field[A_TILES:QUARTER] = total.astype(BF16)
    spread(field, hold1, 1, 0)

    def both(x):
        x = jnp.broadcast_to(x, (8, 128))
        return x + pltpu.roll(x, 64, 1)

    def offer(buf, tile, n):
        buf[mp] = tile
        copies = [
            remote(buf.at[mp], buf.at[mp], s_send.at[n, j - 1], s_recv.at[n, j - 1], (dp, (mp + j) % 4))
            for j in range(1, 4)
        ]
        for copy in copies:
            copy.start()
        return copies

    def collect(buf, n):
        for j in range(1, 4):
            bytes_of(buf.at[(mp + 4 - j) % 4], s_recv.at[n, j - 1])

    def local_stats(x):
        mean = both(jnp.sum(x, axis=0, keepdims=True)) / COUNT
        dev = x - mean[0:1]
        square = both(jnp.sum(dev * dev, axis=0, keepdims=True))
        return jnp.concatenate([mean, square], axis=0)

    def whole_stats(buf, count):
        means = [buf[q, 0:1, :] for q in range(4)]
        mean = (means[0] + means[1] + means[2] + means[3]) * 0.25
        square = jnp.zeros((1, 128), F32)
        for q in range(4):
            off = means[q] - mean
            square = square + buf[q, 8:9, :] + count * (off * off)
        return mean, square / (4.0 * count)

    def pieces(v):
        a = v.astype(BF16).astype(F32)
        b = (v - a).astype(BF16).astype(F32)
        return [a, b, v - a - b]

    x = field[0:QUARTER].reshape(16 * QUARTER, 128).astype(F32)
    half_count = COUNT / 2.0
    mean = jnp.sum(x, axis=0, keepdims=True) / half_count
    dev = x - mean
    square = jnp.sum(dev * dev, axis=0, keepdims=True)
    tile = jnp.concatenate([jnp.broadcast_to(mean, (8, 128)), jnp.broadcast_to(square, (8, 128))], axis=0)
    sent_stats = offer(stat1, tile, 0)
    collect(stat1, 0)
    mean, var = whole_stats(stat1, half_count)

    def stat_tile(values):
        tile = jnp.zeros((16, 128), F32)
        for r, v in enumerate(values):
            tile = jnp.where(q_row == r, v, tile)
        return tile.astype(BF16)

    field[QUARTER] = stat_tile(pieces(mean) + pieces(var))
    spread_stats(field, hold1, 0)

    for n, buf in enumerate((conv_w, exp_w, vecs)):
        shared(buf, sent, n)
    conv_blocks = []
    for dy in range(3):
        w = jnp.concatenate([conv_w[q, dy] for q in range(4)] * 2, axis=0).astype(F32)
        conv_blocks.append(jnp.where(same, w, 0.0).astype(BF16))
    vec_all = vecs[0] + vecs[1] + vecs[2] + vecs[3]
    holder = jnp.logical_or(jnp.logical_or(holds_a, holds_b), holds_s)
    held = jnp.where(holds_s, QUARTER, jnp.where(holds_a, pair, pair + A_TILES))
    held_part = jnp.where(holds_s, 2, jnp.where(holds_a, 0, 1))
    permute(hold1, perm, out1, group, 0, holder, held, held_part)
    arrived(group, 0, 0)
    arrived(group, 0, 1)
    halos = [
        remote(group.at[pl.ds(0, 4)], halo_bottom, halo_send.at[0], halo_recv.at[0], to_l),
        remote(group.at[pl.ds(QUARTER - 4, 4)], halo_top, halo_send.at[1], halo_recv.at[1], to_r),
    ]
    for copy in halos:
        copy.start()
    arrived(group, 0, 2)


    marks = group[QUARTER].astype(F32)
    mean_i = marks[0:1] + marks[1:2] + marks[2:3]
    var_i = marks[3:4] + marks[4:5] + marks[5:6]
    mean = (both(mean_i) * 0.5)[0:1]
    off = mean_i - mean
    var = (both(var_i + off * off) * 0.5)[0:1]
    scale = lax.rsqrt(var + 1e-05)

    def norm1(tiles):
        x = tiles.reshape(-1, 128).astype(F32)
        return jnp.maximum((x - mean) * scale * vec_all[0:1] + vec_all[1:2], 0.0)

    inner = norm1(group[0:QUARTER]).reshape(LINES, SIDE, 128)
    for copy in halos:
        copy.wait_recv()
    top = norm1(halo_top[...])[8:64]
    bottom = norm1(halo_bottom[...])[0:SIDE]
    top = jnp.where(jnp.full((SIDE, 128), mp, jnp.int32) == 0, 0.0, top).reshape(1, SIDE, 128)
    bottom = jnp.where(jnp.full((SIDE, 128), mp, jnp.int32) == 3, 0.0, bottom).reshape(1, SIDE, 128)
    first = jnp.concatenate([top, inner, bottom], axis=0)
    first = jnp.concatenate([first, jnp.zeros((LINES + 2, COLS - SIDE, 128), F32)], axis=1)
    first = first.reshape((LINES + 2) * COLS, 128)

    wide = jnp.concatenate(
        [
            pltpu.roll(first, 1, 0).astype(BF16),
            first.astype(BF16),
            pltpu.roll(first, (LINES + 2) * COLS - 1, 0).astype(BF16),
        ],
        axis=1,
    )
    n_out = LINES * COLS
    spatial = nt(wide[0:n_out], conv_blocks[0])
    spatial = spatial + nt(wide[COLS : COLS + n_out], conv_blocks[1])
    spatial = spatial + nt(wide[2 * COLS : 2 * COLS + n_out], conv_blocks[2])
    spatial = spatial.reshape(LINES, COLS, 128)[:, :SIDE, :].reshape(16 * QUARTER, 128)

    sent_stats += offer(stat2, local_stats(spatial), 1)
    collect(stat2, 1)
    mean, var = whole_stats(stat2, COUNT)
    second = jnp.maximum((spatial - mean) * lax.rsqrt(var + 1e-05) * vec_all[2:3] + vec_all[3:4], 0.0).astype(BF16)
    mid[0:QUARTER] = second.reshape(QUARTER, 16, 128)
    spread(mid, hold2, 0, 1)
    spread(mid, hold2, 1, 1)

    copies3 = []
    for q in range(4):
        stat3s[q] = local_stats(nt(second, diagonal(exp_w[q].astype(F32))))
    for j in range(1, 4):
        q = (mp + j) % 4
        copy = remote(stat3s.at[q], stat3.at[mp], s_send.at[2, j - 1], s_recv.at[2, j - 1], (dp, q))
        copy.start()
        copies3.append(copy)
    stat3[mp] = stat3s[mp]
    sent_stats += copies3
    collect(stat3, 2)
    mean, var = whole_stats(stat3, COUNT)
    mid[QUARTER] = stat_tile(pieces(mean) + pieces(lax.rsqrt(var + 1e-05)))
    spread_stats(mid, hold2, 1)
    permute(hold2, inv, out2, home, 1, holder, held, held_part)

    def a_of(q):
        return second_all.at[pl.ds(QUARTER * q, A_TILES)]

    def b_of(q):
        return second_all.at[pl.ds(QUARTER * q + A_TILES, B_TILES)]

    ag = [
        remote(a_of(mp), a_of(mp), ag_send.at[0], ag_recv.at[0], to_r),
        remote(a_of(mp), a_of(mp), ag_send.at[1], ag_recv.at[1], to_l),
        remote(b_of(mp), b_of(mp), ag_send.at[2], ag_recv.at[2], to_l),
        remote(b_of(mp), b_of(mp), ag_send.at[3], ag_recv.at[3], to_r),
        remote(a_of(left), a_of(left), ag_send.at[4], ag_recv.at[4], to_r),
        remote(b_of(right), b_of(right), ag_send.at[5], ag_recv.at[5], to_l),
    ]
    arrived(home, 1, 0)
    second_all[pl.ds(QUARTER * mp, A_TILES)] = home[0:A_TILES]
    ag[0].start()
    ag[1].start()
    arrived(home, 1, 1)
    second_all[pl.ds(QUARTER * mp + A_TILES, B_TILES)] = home[A_TILES:QUARTER]
    ag[2].start()
    ag[3].start()
    bytes_of(a_of(left), ag_recv.at[0])
    ag[4].start()
    bytes_of(b_of(right), ag_recv.at[2])
    ag[5].start()
    arrived(home, 1, 2)

    identity = jnp.where(
        lax.broadcasted_iota(jnp.int32, (128, 128), 0) == lax.broadcasted_iota(jnp.int32, (128, 128), 1),
        1.0,
        0.0,
    ).astype(BF16)
    columns = nt(identity, home[QUARTER])
    mean_c = columns[:, 0:1] + columns[:, 1:2] + columns[:, 2:3]
    scale_c = columns[:, 3:4] + columns[:, 4:5] + columns[:, 5:6]

    def expand(block, lanes):
        v = nt(we_block, block)
        third = ((v - mean_c) * scale_c * gain_c + shift_c).astype(BF16).astype(F32)
        f = jnp.maximum(third + img[:, lanes].astype(F32), 0.0).astype(BF16)
        feat[:, lanes] = f
        return f.astype(F32)

    def expand_at(i, pooled):
        j = ((QUARTER * far + QUARTER - 1) // 32 + 1 + i) % 6
        block = second_all[pl.ds(32 * j, 32)].reshape(512, 128)
        f = expand(block, pl.ds(pl.multiple_of(512 * j, 512), 512))
        return pooled + (f[:, 0:128] + f[:, 128:256] + f[:, 256:384] + f[:, 384:512])

    bytes_of(a_of(right), ag_recv.at[1])
    bytes_of(b_of(left), ag_recv.at[3])
    pooled = jnp.zeros((128, 128), F32)
    for i in range(3):
        pooled = expand_at(i, pooled)
    bytes_of(a_of(far), ag_recv.at[4])
    bytes_of(b_of(far), ag_recv.at[5])
    for i in range(3, 6):
        pooled = expand_at(i, pooled)
    rest = expand(second_all[192:196].reshape(64, 128), slice(3072, 3136))
    write = pltpu.make_async_copy(feat, feat_hbm, feat_sem)
    write.start()
    pooled = jnp.sum(pooled, axis=1, keepdims=True) + jnp.sum(rest, axis=1, keepdims=True)
    pooled = pooled / float(PIXELS)

    proj2 = jnp.concatenate([proj[...], proj[...]], axis=0).astype(F32)
    terms = pooled * proj2
    e0 = jnp.sum(terms[0:64], axis=0, keepdims=True)
    e1 = jnp.sum(terms[64:128], axis=0, keepdims=True)
    row8 = lax.broadcasted_iota(jnp.int32, (8, 128), 0)
    top = jnp.where(row8 == 0, e0, jnp.where(row8 == 1, e1, 0.0))
    emb[core, mp] = jnp.concatenate([top, mass[0:8]], axis=0)
    mine = emb.at[core, mp]
    e_copies = []
    for j in range(1, 4):
        e_copies.append(remote(mine, mine, e_send.at[j], e_recv.at[j], (dp, (mp + j) % 4)))
    for j in range(4):
        e_copies.append(remote(mine, mine, e_send.at[4 + j], e_recv.at[4 + j], (other, (mp + j) % 4)))
    for copy in e_copies:
        copy.start()
    for j in range(1, 4):
        bytes_of(emb.at[core, (mp + 4 - j) % 4], e_recv.at[j])
    for j in range(4):
        bytes_of(emb.at[1 - core, (mp + 4 - j) % 4], e_recv.at[4 + j])

    key_tile = jnp.zeros((16, 128), F32)
    for cc in range(2):
        e = emb[cc, 0, 0:8] + emb[cc, 1, 0:8] + emb[cc, 2, 0:8] + emb[cc, 3, 0:8]
        key = e * lax.rsqrt(jnp.sum(e * e, axis=1, keepdims=True) + 1e-06)
        for b in range(2):
            here = q_row == 4 * (me % 4) + 2 * cc + b
            key_tile = jnp.where(here, key[b : b + 1], key_tile)
    queue = emb[core, 0, 8:16] + emb[core, 1, 8:16] + emb[core, 2, 8:16] + emb[core, 3, 8:16]
    z = me % 8
    slab = me // 8
    keys1[z] = key_tile.astype(BF16)
    k_copies = []
    for j in range(1, 8):
        h = slab * 8 + (z + j) % 8
        k_copies.append(remote(keys1.at[z], keys1.at[z], k_send.at[0, j], k_recv.at[0, j], (h * 2 + core, mp)))
    for copy in k_copies:
        copy.start()
    for j in range(1, 8):
        bytes_of(keys1.at[(z + 8 - j) % 8], k_recv.at[0, j])
    keys2[slab] = jnp.sum(keys1[...].astype(F32).reshape(2, 4, 16, 128), axis=1).astype(BF16)
    k_copies2 = []
    for j in range(1, 8):
        h = (me + 8 * j) % CHIPS
        k_copies2.append(
            remote(keys2.at[slab], keys2.at[slab], k_send.at[1, j], k_recv.at[1, j], (h * 2 + core, mp))
        )
    for copy in k_copies2:
        copy.start()
    for j in range(1, 8):
        bytes_of(keys2.at[(slab + 8 - j) % 8], k_recv.at[1, j])
    every = keys2[...].reshape(256, 128)
    score = (nt(unit, every) / DIVISOR)[0:8]
    score_out[...] = score[0:2]
    lane = lax.broadcasted_iota(jnp.int32, (8, 256), 1)
    row = lax.broadcasted_iota(jnp.int32, (8, 256), 0)
    matched = jnp.sum(jnp.where(lane == 2 * dp + row, score, 0.0), axis=1, keepdims=True)
    mass_all = jnp.sum(jnp.exp(score), axis=1, keepdims=True) + queue[:, 0:1]
    losses = jnp.broadcast_to(jnp.log(mass_all) - matched, (8, 128))
    lane8 = lax.broadcasted_iota(jnp.int32, (8, 128), 1)
    loss_out[...] = jnp.sum(jnp.where(row8 == lane8, losses, 0.0), axis=0, keepdims=True)[:, 0:2]

    write.wait()
    for copy in rs + sent + sent_stats + ag + halos + e_copies + k_copies + k_copies2:
        copy.wait_send()
    for slot, (src, out) in enumerate(((field, out1), (mid, out2))):

        @pl.when(holder)
        def _():
            bytes_of(src.at[pl.ds(0, BACK - 1)], hop_send.at[slot])
            bytes_of(out.at[pl.ds(0, CHIPS - 1)], out_send.at[slot])

        @pl.when(jnp.logical_not(holder))
        def _():
            bytes_of(src, hop_send.at[slot])


def on_device(
    images,
    permutation,
    inverse,
    reduce_weight,
    reduce_gain,
    reduce_shift,
    spatial_weight,
    spatial_gain,
    spatial_shift,
    expand_weight,
    expand_gain,
    expand_shift,
    projection,
    queries,
    dictionary_bank,
):
    cw = jnp.transpose(spatial_weight, (2, 3, 0, 1))
    rows = [
        v.reshape(1, -1)
        for v in (reduce_gain, reduce_shift, spatial_gain, spatial_shift, expand_gain, expand_shift)
    ]

    vmem = pl.BlockSpec(memory_space=pltpu.VMEM)
    smem = pl.BlockSpec(memory_space=pltpu.SMEM)
    dma = pltpu.SemaphoreType.DMA
    feat, score, loss = pl.pallas_call(
        kernel,
        out_shape=(
            jax.ShapeDtypeStruct((128, PIXELS), BF16),
            jax.ShapeDtypeStruct((2, 256), F32),
            jax.ShapeDtypeStruct((1, 2), F32),
        ),
        in_specs=[smem, smem, pl.BlockSpec(memory_space=pl.ANY)] + [vmem] * 12,
        out_specs=(pl.BlockSpec(memory_space=pl.ANY), vmem, vmem),
        scratch_shapes=[
            pltpu.VMEM((128, PIXELS), BF16),
            pltpu.VMEM((128, PIXELS), BF16),
            pltpu.VMEM((4 * QUARTER, 16, 128), BF16),
            pltpu.VMEM((QUARTER, 16, 128), BF16),
            pltpu.VMEM((QUARTER, 16, 128), BF16),
            pltpu.VMEM((A_TILES, 16, 128), BF16),
            pltpu.VMEM((B_TILES, 16, 128), BF16),
            pltpu.VMEM((A_TILES, 16, 128), BF16),
            pltpu.VMEM((B_TILES, 16, 128), BF16),
            pltpu.VMEM((4, 3, 16, 384), BF16),
            pltpu.VMEM((4, 64, 128), BF16),
            pltpu.VMEM((4, 8, 128), F32),
            pltpu.VMEM((BACK, 16, 128), BF16),
            pltpu.VMEM((CHIPS, 2, 2, 16, 128), BF16),
            pltpu.VMEM((CHIPS, 16, 128), BF16),
            pltpu.VMEM((BACK, 16, 128), BF16),
            pltpu.VMEM((4, 16, 128), F32),
            pltpu.VMEM((4, 16, 128), F32),
            pltpu.VMEM((4, 16, 128), F32),
            pltpu.VMEM((4, 16, 128), F32),
            pltpu.VMEM((BACK, 16, 128), BF16),
            pltpu.VMEM((CHIPS, 2, 2, 16, 128), BF16),
            pltpu.VMEM((CHIPS, 16, 128), BF16),
            pltpu.VMEM((BACK, 16, 128), BF16),
            pltpu.VMEM((4 * QUARTER, 16, 128), BF16),
            pltpu.VMEM((2, 4, 16, 128), F32),
            pltpu.VMEM((8, 16, 128), BF16),
            pltpu.VMEM((8, 2, 16, 128), BF16),
            pltpu.VMEM((4, 16, 128), BF16),
            pltpu.VMEM((4, 16, 128), BF16),
            dma,
            dma,
            dma((6,)),
            dma((6,)),
            dma((3, 3)),
            dma((3, 3)),
            dma((3, 3)),
            dma((3, 3)),
            dma((2,)),
            dma((2, 8)),
            dma((2,)),
            dma((2, 3)),
            dma((2,)),
            dma((2,)),
            dma((2, 8)),
            dma((2, 8)),
            dma((6,)),
            dma((6,)),
            dma((8,)),
            dma((8,)),
            dma((2, 8)),
            dma((2, 8)),
        ],
        compiler_params=pltpu.CompilerParams(
            collective_id=0, has_side_effects=True, vmem_limit_bytes=63 * 1024 * 1024
        ),
        cost_estimate=pl.CostEstimate(
            flops=2 * 3136 * 128 * 128 * 4, bytes_accessed=2 * 128 * 3136 * 2, transcendentals=0
        ),
    )(
        permutation,
        inverse,
        images.reshape(128, PIXELS),
        reduce_weight,
        cw,
        expand_weight,
        *rows,
        projection,
        queries,
        dictionary_bank,
    )
    return feat.reshape(images.shape), score, loss.reshape(2)


def solution(mesh):
    placed = (
        P("dp", "mp", None),
        P(),
        P(),
        P(None, "mp"),
        P("mp"),
        P("mp"),
        P("mp", None, None, None),
        P("mp"),
        P("mp"),
        P("mp", None),
        P("mp"),
        P("mp"),
        P("mp", None),
        P("dp", None),
        P("mp", None),
    )
    return jax.shard_map(
        on_device,
        mesh=mesh,
        in_specs=placed,
        out_specs=(P("dp", "mp", None), P("dp", None), P("dp")),
        check_vma=False,
    )
```

```python
import jax
import jax.numpy as jnp
from jax import lax
from jax.experimental import pallas as pl
from jax.experimental.pallas import tpu as pltpu
from jax.sharding import PartitionSpec as P

MESH = pl.DeviceIdType.MESH
F32 = jnp.float32
BF16 = jnp.bfloat16

SIDE = 56
PIXELS = SIDE * SIDE
COLS = 64
CHIPS = 64
LINES = SIDE // 4
QUARTER = PIXELS // 4 // 16
A_TILES = 25
B_TILES = QUARTER - A_TILES
B_EARLY = 8
BACK = QUARTER + 1
STAT_CHIP = CHIPS - 1
COUNT = 2.0 * (PIXELS // 4)
DIVISOR = 0.2


def nt(a, b):
    return lax.dot_general(a, b, (((1,), (1,)), ((), ())), preferred_element_type=F32)


def tn(a, b):
    return lax.dot_general(a, b, (((0,), (1,)), ((), ())), preferred_element_type=F32)


def remote(src, dst, send, recv, device):
    return pltpu.make_async_remote_copy(
        src_ref=src,
        dst_ref=dst,
        send_sem=send,
        recv_sem=recv,
        device_id=device,
        device_id_type=MESH,
    )


def bytes_of(ref, sem):
    pltpu.make_async_copy(ref, ref, sem).wait()


def kernel(
    perm,
    inv,
    img_hbm,
    rw,
    cw,
    we,
    rg,
    rsh,
    sg,
    ssh,
    eg,
    esh,
    proj,
    queries,
    bank,
    feat_hbm,
    score_out,
    loss_out,
    img,
    feat,
    part,
    from_left,
    from_right,
    via_left,
    via_right,
    sum_a,
    sum_b,
    conv_w,
    exp_w,
    vecs,
    field,
    hold1,
    out1,
    group,
    stat1,
    stat2,
    stat3s,
    stat3,
    mid,
    hold2,
    out2,
    home,
    second_all,
    emb,
    keys1,
    keys2,
    halo_top,
    halo_bottom,
    img_sem,
    feat_sem,
    rs_send,
    rs_recv,
    w_send,
    w_recv,
    s_send,
    s_recv,
    hop_send,
    hop_recv,
    out_send,
    out_recv,
    halo_send,
    halo_recv,
    pair_send,
    pair_recv,
    ag_send,
    ag_recv,
    e_send,
    e_recv,
    k_send,
    k_recv,
):
    dp = lax.axis_index("dp")
    mp = lax.axis_index("mp")
    me = dp // 2
    core = dp % 2
    other = dp + 1 - 2 * core
    right = (mp + 1) % 4
    left = (mp + 3) % 4
    far = (mp + 2) % 4

    fetch = pltpu.make_async_copy(img_hbm, img, img_sem)
    fetch.start()

    barrier = pltpu.get_barrier_semaphore()

    def greet(i, carry):
        for u in range(7):
            h = (me + 1 + 7 * i + u) % CHIPS
            pl.semaphore_signal(barrier, inc=1, device_id=(h * 2 + core, mp), device_id_type=MESH)
        return carry

    for j in range(1, 4):
        pl.semaphore_signal(barrier, inc=1, device_id=(dp, (mp + j) % 4), device_id_type=MESH)
    for j in range(4):
        pl.semaphore_signal(barrier, inc=1, device_id=(other, (mp + j) % 4), device_id_type=MESH)
    lax.fori_loop(0, 9, greet, 0)

    row128 = lax.broadcasted_iota(jnp.int32, (128, 384), 0) // 64
    lane128 = (lax.broadcasted_iota(jnp.int32, (128, 384), 1) // 64) % 2
    same = row128 == lane128
    eye_block = same[:, 0:128]

    def doubled(w):
        w = w.astype(F32)
        return jnp.concatenate([w, w], axis=1)

    def diagonal(w):
        return jnp.where(eye_block, jnp.concatenate([w, w], axis=0), 0.0).astype(BF16)

    rw_block = diagonal(doubled(rw[...]))
    fetch.wait()

    for k in range(5):
        n = 40 if k < 4 else 36
        block = tn(img[:, 640 * k : 640 * k + 16 * n], rw_block)
        part[40 * k : 40 * k + n] = block.astype(BF16).reshape(n, 16, 128)

    pl.semaphore_wait(barrier, CHIPS - 1 + 7)

    def a_part(q):
        return part.at[pl.ds(QUARTER * q, A_TILES)]

    def b_part(q):
        return part.at[pl.ds(QUARTER * q + A_TILES, B_TILES)]

    to_r = (dp, right)
    to_l = (dp, left)
    left_a = from_left.at[pl.ds(0, A_TILES)]
    left_b = from_left.at[pl.ds(A_TILES, B_TILES)]
    right_a = from_right.at[pl.ds(0, A_TILES)]
    right_b = from_right.at[pl.ds(A_TILES, B_TILES)]
    b_first = part.at[pl.ds(QUARTER * right + A_TILES, B_EARLY)]
    b_later = part.at[pl.ds(QUARTER * right + A_TILES + B_EARLY, B_TILES - B_EARLY)]
    left_b_first = from_left.at[pl.ds(A_TILES, B_EARLY)]
    left_b_later = from_left.at[pl.ds(A_TILES + B_EARLY, B_TILES - B_EARLY)]
    rs = [
        remote(a_part(far), via_left, rs_send.at[0], rs_recv.at[0], to_r),
        remote(b_part(far), via_right, rs_send.at[3], rs_recv.at[3], to_l),
        remote(b_first, left_b_first, rs_send.at[2], rs_recv.at[2], to_r),
        remote(a_part(left), right_a, rs_send.at[1], rs_recv.at[1], to_l),
        remote(sum_a, left_a, rs_send.at[4], rs_recv.at[4], to_r),
        remote(b_later, left_b_later, rs_send.at[6], rs_recv.at[6], to_r),
        remote(sum_b, right_b, rs_send.at[5], rs_recv.at[5], to_l),
    ]
    for copy in rs[:4]:
        copy.start()

    vin = jnp.concatenate([rg[...], rsh[...], sg[...], ssh[...], eg[...], esh[...]], axis=1)
    we_wide = doubled(we[...])
    we_block = diagonal(we_wide)
    v_row = lax.broadcasted_iota(jnp.int32, (8, 192), 0)
    v_lane = lax.broadcasted_iota(jnp.int32, (8, 192), 1)
    v_in = jnp.where(v_lane // 16 == v_row, jnp.broadcast_to(vin, (8, 192)), 0.0)
    v_in = jnp.where(v_row < 4, v_in, 0.0)
    p_row = lax.broadcasted_iota(jnp.int32, (192, 128), 0)
    p_lane = lax.broadcasted_iota(jnp.int32, (192, 128), 1)
    v_place = jnp.where(p_row % 16 + 16 * mp == p_lane % 64, 1.0, 0.0)
    vec = jnp.dot(v_in, v_place, precision=lax.Precision.HIGHEST, preferred_element_type=F32)
    c_row = lax.broadcasted_iota(jnp.int32, (128, 192), 0) % 64
    c_lane = lax.broadcasted_iota(jnp.int32, (128, 192), 1)
    v_all = jnp.broadcast_to(vin, (128, 192))
    gain_c = jnp.sum(jnp.where(c_lane == c_row + 64, v_all, 0.0), axis=1, keepdims=True)
    shift_c = jnp.sum(jnp.where(c_lane == c_row + 128, v_all, 0.0), axis=1, keepdims=True)
    for dy in range(3):
        conv_w[mp, dy] = jnp.concatenate([doubled(cw[dy, dx]) for dx in range(3)], axis=1).astype(BF16)
    exp_w[mp] = we_wide.astype(BF16)
    vecs[mp] = vec

    def share(buf, n):
        copies = [
            remote(buf.at[mp], buf.at[mp], w_send.at[n, j - 1], w_recv.at[n, j - 1], (dp, (mp + j) % 4))
            for j in range(1, 4)
        ]
        for copy in copies:
            copy.start()
        return copies

    def shared(buf, copies, n):
        for j in range(1, 4):
            src = buf.at[(mp + 4 - j) % 4]
            bytes_of(src, w_recv.at[n, j - 1])

    sent = []

    q_row = lax.broadcasted_iota(jnp.int32, (16, 128), 0)
    q_all = jnp.where(q_row == 0, queries[0:1, :], jnp.where(q_row == 1, queries[1:2, :], 0.0))
    unit = (q_all * lax.rsqrt(jnp.sum(q_all * q_all, axis=1, keepdims=True) + 1e-06)).astype(BF16)
    stored = nt(unit, bank[...]) / DIVISOR
    mass = jnp.broadcast_to(jnp.sum(jnp.exp(stored), axis=1, keepdims=True), (16, 128))

    rs[0].wait_recv()
    own = part[pl.ds(QUARTER * right, A_TILES)].astype(F32)
    sum_a[...] = (own + via_left[...].astype(F32)).astype(BF16)
    rs[4].start()
    rs[5].start()
    rs[1].wait_recv()
    own = part[pl.ds(QUARTER * left + A_TILES, B_TILES)].astype(F32)
    sum_b[...] = (own + via_right[...].astype(F32)).astype(BF16)
    rs[6].start()

    sent += share(conv_w, 0)
    sent += share(exp_w, 1)
    sent += share(vecs, 2)

    low = lax.broadcasted_iota(jnp.int32, (16, 128), 1) < 64
    pair = me // 2
    holds_a = jnp.logical_and(me % 2 == 0, pair < A_TILES)
    holds_b = jnp.logical_and(me % 2 == 1, pair < B_TILES)
    holds_s = me == STAT_CHIP

    def send_tile(src, t, hold, h, slot):
        remote(
            src.at[t],
            hold.at[me, core, 0],
            hop_send.at[slot],
            hop_recv.at[slot, me // 8],
            (h * 2 + core, mp),
        ).start()

    def spread(src, hold, odd, slot):
        n = B_TILES if odd else A_TILES

        def step(i, carry):
            for u in range(8):
                t = (pair + 8 * i + u) % (CHIPS // 2)
                h = 2 * t + odd

                @pl.when(jnp.logical_and(h != me, t < n))
                def _():
                    send_tile(src, t + odd * A_TILES, hold, h, slot)

            return carry

        lax.fori_loop(0, 4, step, 0)

        @pl.when(holds_b if odd else holds_a)
        def _():
            hold[me, core, 0] = src[pair + odd * A_TILES]

    def spread_stats(src, hold, slot):
        @pl.when(me != STAT_CHIP)
        def _():
            send_tile(src, QUARTER, hold, STAT_CHIP, slot)

        @pl.when(holds_s)
        def _():
            hold[STAT_CHIP, core, 0] = src[QUARTER]

    def permute(hold, order, out, dst, slot, holds, tile, part_of):
        def turn(side, g):
            at = pl.ds(8 * g, 8)
            x = hold[at, side, 0].reshape(128, 128).astype(F32)
            hold[at, side, 1] = pltpu.roll(x, 64, 1).astype(BF16).reshape(8, 16, 128)

        def swapping(g):
            ref = hold.at[pl.ds(8 * g, 8), core, 0]
            return remote(ref, ref, pair_send.at[slot, g], pair_recv.at[slot, g], (other, mp))

        def take(i, carry):
            g = (me // 8 + 8 - i) % 8
            bytes_of(hold.at[pl.ds(8 * g, 8), core, 0], hop_recv.at[slot, g])
            swapping(g).start()
            turn(core, g)
            return carry

        def take_other(i, carry):
            g = (me // 8 + 16 - i) % 8
            bytes_of(hold.at[pl.ds(8 * g, 8), 1 - core, 0], pair_recv.at[slot, g])
            turn(1 - core, g)
            return carry

        def swapped(i, carry):
            swapping(i).wait_send()
            return carry

        def pick(t):
            at = 4 * t + 2 * core
            i0 = order[at]
            i1 = order[at + 1]
            x0 = hold[i0 >> 2, (i0 >> 1) & 1, i0 & 1]
            x1 = hold[i1 >> 2, (i1 >> 1) & 1, 1 - (i1 & 1)]
            return jnp.where(low, x0, x1)

        @pl.when(holds)
        def _():
            lax.fori_loop(1, 8, take, 0)
            g = me // 8
            bytes_of(hold.at[pl.ds(8 * g, 7), core, 0], hop_recv.at[slot, g])
            swapping(g).start()
            turn(core, g)
            lax.fori_loop(1, 9, take_other, 0)

            def step(i, carry):
                ts = [(me + 1 + 9 * i + u) % CHIPS for u in range(9)]
                values = [pick(t) for t in ts]
                for t, value in zip(ts, values):
                    out[t] = value
                for t in ts:
                    remote(
                        out.at[t],
                        dst.at[tile],
                        out_send.at[slot],
                        out_recv.at[slot, part_of],
                        (t * 2 + core, mp),
                    ).start()
                return carry

            lax.fori_loop(0, 7, step, 0)
            dst[tile] = pick(me)
            lax.fori_loop(0, 8, swapped, 0)

    def arrived(dst, slot, part_of):
        start, n, holds = ((0, A_TILES, holds_a), (A_TILES, B_TILES, holds_b), (QUARTER, 1, holds_s))[part_of]

        @pl.when(jnp.logical_not(holds))
        def _():
            bytes_of(dst.at[pl.ds(start, n)], out_recv.at[slot, part_of])

        if n > 1:

            @pl.when(holds)
            def _():
                bytes_of(dst.at[pl.ds(start, n - 1)], out_recv.at[slot, part_of])

    rs[4].wait_recv()
    rs[3].wait_recv()
    total = part[pl.ds(QUARTER * mp, A_TILES)].astype(F32)
    total = total + left_a[...].astype(F32) + right_a[...].astype(F32)
    field[0:A_TILES] = total.astype(BF16)
    spread(field, hold1, 0, 0)

    for copy in (rs[2], rs[5], rs[6]):
        copy.wait_recv()
    total = part[pl.ds(QUARTER * mp + A_TILES, B_TILES)].astype(F32)
    total = total + left_b[...].astype(F32) + right_b[...].astype(F32)
    field[A_TILES:QUARTER] = total.astype(BF16)
    spread(field, hold1, 1, 0)

    def both(x):
        x = jnp.broadcast_to(x, (8, 128))
        return x + pltpu.roll(x, 64, 1)

    def offer(buf, tile, n):
        buf[mp] = tile
        copies = [
            remote(buf.at[mp], buf.at[mp], s_send.at[n, j - 1], s_recv.at[n, j - 1], (dp, (mp + j) % 4))
            for j in range(1, 4)
        ]
        for copy in copies:
            copy.start()
        return copies

    def collect(buf, n):
        for j in range(1, 4):
            bytes_of(buf.at[(mp + 4 - j) % 4], s_recv.at[n, j - 1])

    def local_stats(x):
        mean = both(jnp.sum(x, axis=0, keepdims=True)) / COUNT
        dev = x - mean[0:1]
        square = both(jnp.sum(dev * dev, axis=0, keepdims=True))
        return jnp.concatenate([mean, square], axis=0)

    def whole_stats(buf, count):
        means = [buf[q, 0:1, :] for q in range(4)]
        mean = (means[0] + means[1] + means[2] + means[3]) * 0.25
        square = jnp.zeros((1, 128), F32)
        for q in range(4):
            off = means[q] - mean
            square = square + buf[q, 8:9, :] + count * (off * off)
        return mean, square / (4.0 * count)

    def pieces(v):
        a = v.astype(BF16).astype(F32)
        b = (v - a).astype(BF16).astype(F32)
        return [a, b, v - a - b]

    x = field[0:QUARTER].reshape(16 * QUARTER, 128).astype(F32)
    half_count = COUNT / 2.0
    mean = jnp.sum(x, axis=0, keepdims=True) / half_count
    dev = x - mean
    square = jnp.sum(dev * dev, axis=0, keepdims=True)
    tile = jnp.concatenate([jnp.broadcast_to(mean, (8, 128)), jnp.broadcast_to(square, (8, 128))], axis=0)
    sent_stats = offer(stat1, tile, 0)
    collect(stat1, 0)
    mean, var = whole_stats(stat1, half_count)

    def stat_tile(values):
        tile = jnp.zeros((16, 128), F32)
        for r, v in enumerate(values):
            tile = jnp.where(q_row == r, v, tile)
        return tile.astype(BF16)

    field[QUARTER] = stat_tile(pieces(mean) + pieces(var))
    spread_stats(field, hold1, 0)

    holder = jnp.logical_or(jnp.logical_or(holds_a, holds_b), holds_s)
    held = jnp.where(holds_s, QUARTER, jnp.where(holds_a, pair, pair + A_TILES))
    held_part = jnp.where(holds_s, 2, jnp.where(holds_a, 0, 1))
    permute(hold1, perm, out1, group, 0, holder, held, held_part)
    for n, buf in enumerate((conv_w, exp_w, vecs)):
        shared(buf, sent, n)
    conv_blocks = []
    for dy in range(3):
        w = jnp.concatenate([conv_w[q, dy] for q in range(4)] * 2, axis=0).astype(F32)
        conv_blocks.append(jnp.where(same, w, 0.0).astype(BF16))
    vec_all = vecs[0] + vecs[1] + vecs[2] + vecs[3]
    arrived(group, 0, 0)
    arrived(group, 0, 1)
    halos = [
        remote(group.at[pl.ds(0, 4)], halo_bottom, halo_send.at[0], halo_recv.at[0], to_l),
        remote(group.at[pl.ds(QUARTER - 4, 4)], halo_top, halo_send.at[1], halo_recv.at[1], to_r),
    ]
    for copy in halos:
        copy.start()
    arrived(group, 0, 2)


    marks = group[QUARTER].astype(F32)
    mean_i = marks[0:1] + marks[1:2] + marks[2:3]
    var_i = marks[3:4] + marks[4:5] + marks[5:6]
    mean = (both(mean_i) * 0.5)[0:1]
    off = mean_i - mean
    var = (both(var_i + off * off) * 0.5)[0:1]
    scale = lax.rsqrt(var + 1e-05)

    def norm1(tiles):
        x = tiles.reshape(-1, 128).astype(F32)
        return jnp.maximum((x - mean) * scale * vec_all[0:1] + vec_all[1:2], 0.0)

    inner = norm1(group[0:QUARTER]).reshape(LINES, SIDE, 128)
    for copy in halos:
        copy.wait_recv()
    top = norm1(halo_top[...])[8:64]
    bottom = norm1(halo_bottom[...])[0:SIDE]
    top = jnp.where(jnp.full((SIDE, 128), mp, jnp.int32) == 0, 0.0, top).reshape(1, SIDE, 128)
    bottom = jnp.where(jnp.full((SIDE, 128), mp, jnp.int32) == 3, 0.0, bottom).reshape(1, SIDE, 128)
    first = jnp.concatenate([top, inner, bottom], axis=0)
    first = jnp.concatenate([first, jnp.zeros((LINES + 2, COLS - SIDE, 128), F32)], axis=1)
    first = first.reshape((LINES + 2) * COLS, 128)

    wide = jnp.concatenate(
        [
            pltpu.roll(first, 1, 0).astype(BF16),
            first.astype(BF16),
            pltpu.roll(first, (LINES + 2) * COLS - 1, 0).astype(BF16),
        ],
        axis=1,
    )
    n_out = LINES * COLS
    spatial = nt(wide[0:n_out], conv_blocks[0])
    spatial = spatial + nt(wide[COLS : COLS + n_out], conv_blocks[1])
    spatial = spatial + nt(wide[2 * COLS : 2 * COLS + n_out], conv_blocks[2])
    spatial = spatial.reshape(LINES, COLS, 128)[:, :SIDE, :].reshape(16 * QUARTER, 128)

    sent_stats += offer(stat2, local_stats(spatial), 1)
    collect(stat2, 1)
    mean, var = whole_stats(stat2, COUNT)
    second = jnp.maximum((spatial - mean) * lax.rsqrt(var + 1e-05) * vec_all[2:3] + vec_all[3:4], 0.0).astype(BF16)
    mid[0:QUARTER] = second.reshape(QUARTER, 16, 128)
    spread(mid, hold2, 0, 1)
    spread(mid, hold2, 1, 1)

    copies3 = []
    for q in range(4):
        stat3s[q] = local_stats(nt(second, diagonal(exp_w[q].astype(F32))))
    for j in range(1, 4):
        q = (mp + j) % 4
        copy = remote(stat3s.at[q], stat3.at[mp], s_send.at[2, j - 1], s_recv.at[2, j - 1], (dp, q))
        copy.start()
        copies3.append(copy)
    stat3[mp] = stat3s[mp]
    sent_stats += copies3
    collect(stat3, 2)
    mean, var = whole_stats(stat3, COUNT)
    mid[QUARTER] = stat_tile(pieces(mean) + pieces(lax.rsqrt(var + 1e-05)))
    spread_stats(mid, hold2, 1)
    permute(hold2, inv, out2, home, 1, holder, held, held_part)

    def a_of(q):
        return second_all.at[pl.ds(QUARTER * q, A_TILES)]

    def b_of(q):
        return second_all.at[pl.ds(QUARTER * q + A_TILES, B_TILES)]

    ag = [
        remote(a_of(mp), a_of(mp), ag_send.at[0], ag_recv.at[0], to_r),
        remote(a_of(mp), a_of(mp), ag_send.at[1], ag_recv.at[1], to_l),
        remote(b_of(mp), b_of(mp), ag_send.at[2], ag_recv.at[2], to_l),
        remote(b_of(mp), b_of(mp), ag_send.at[3], ag_recv.at[3], to_r),
        remote(a_of(left), a_of(left), ag_send.at[4], ag_recv.at[4], to_r),
        remote(b_of(right), b_of(right), ag_send.at[5], ag_recv.at[5], to_l),
    ]
    arrived(home, 1, 0)
    second_all[pl.ds(QUARTER * mp, A_TILES)] = home[0:A_TILES]
    ag[0].start()
    arrived(home, 1, 1)
    second_all[pl.ds(QUARTER * mp + A_TILES, B_TILES)] = home[A_TILES:QUARTER]
    ag[2].start()
    ag[3].start()
    ag[1].start()
    bytes_of(a_of(left), ag_recv.at[0])
    ag[4].start()
    bytes_of(b_of(right), ag_recv.at[2])
    ag[5].start()
    arrived(home, 1, 2)

    identity = jnp.where(
        lax.broadcasted_iota(jnp.int32, (128, 128), 0) == lax.broadcasted_iota(jnp.int32, (128, 128), 1),
        1.0,
        0.0,
    ).astype(BF16)
    columns = nt(identity, home[QUARTER])
    mean_c = columns[:, 0:1] + columns[:, 1:2] + columns[:, 2:3]
    scale_c = columns[:, 3:4] + columns[:, 4:5] + columns[:, 5:6]

    def expand(block, lanes):
        v = nt(we_block, block)
        third = ((v - mean_c) * scale_c * gain_c + shift_c).astype(BF16).astype(F32)
        f = jnp.maximum(third + img[:, lanes].astype(F32), 0.0).astype(BF16)
        feat[:, lanes] = f
        return f.astype(F32)

    def expand_at(i, pooled):
        j = ((QUARTER * far + QUARTER - 1) // 32 + 1 + i) % 6
        block = second_all[pl.ds(32 * j, 32)].reshape(512, 128)
        f = expand(block, pl.ds(pl.multiple_of(512 * j, 512), 512))
        return pooled + (f[:, 0:128] + f[:, 128:256] + f[:, 256:384] + f[:, 384:512])

    bytes_of(a_of(right), ag_recv.at[1])
    bytes_of(b_of(left), ag_recv.at[3])
    pooled = jnp.zeros((128, 128), F32)
    for i in range(3):
        pooled = expand_at(i, pooled)
    bytes_of(a_of(far), ag_recv.at[4])
    bytes_of(b_of(far), ag_recv.at[5])
    for i in range(3, 6):
        pooled = expand_at(i, pooled)
    rest = expand(second_all[192:196].reshape(64, 128), slice(3072, 3136))
    write = pltpu.make_async_copy(feat, feat_hbm, feat_sem)
    write.start()
    pooled = jnp.sum(pooled, axis=1, keepdims=True) + jnp.sum(rest, axis=1, keepdims=True)
    pooled = pooled / float(PIXELS)

    proj2 = jnp.concatenate([proj[...], proj[...]], axis=0).astype(F32)
    terms = pooled * proj2
    e0 = jnp.sum(terms[0:64], axis=0, keepdims=True)
    e1 = jnp.sum(terms[64:128], axis=0, keepdims=True)
    row8 = lax.broadcasted_iota(jnp.int32, (8, 128), 0)
    top = jnp.where(row8 == 0, e0, jnp.where(row8 == 1, e1, 0.0))
    emb[core, mp] = jnp.concatenate([top, mass[0:8]], axis=0)
    mine = emb.at[core, mp]
    e_copies = []
    for j in range(1, 4):
        e_copies.append(remote(mine, mine, e_send.at[j], e_recv.at[j], (dp, (mp + j) % 4)))
    for j in range(4):
        e_copies.append(remote(mine, mine, e_send.at[4 + j], e_recv.at[4 + j], (other, (mp + j) % 4)))
    for copy in e_copies:
        copy.start()
    for j in range(1, 4):
        bytes_of(emb.at[core, (mp + 4 - j) % 4], e_recv.at[j])
    for j in range(4):
        bytes_of(emb.at[1 - core, (mp + 4 - j) % 4], e_recv.at[4 + j])

    key_tile = jnp.zeros((16, 128), F32)
    for cc in range(2):
        e = emb[cc, 0, 0:8] + emb[cc, 1, 0:8] + emb[cc, 2, 0:8] + emb[cc, 3, 0:8]
        key = e * lax.rsqrt(jnp.sum(e * e, axis=1, keepdims=True) + 1e-06)
        for b in range(2):
            here = q_row == 4 * (me % 4) + 2 * cc + b
            key_tile = jnp.where(here, key[b : b + 1], key_tile)
    queue = emb[core, 0, 8:16] + emb[core, 1, 8:16] + emb[core, 2, 8:16] + emb[core, 3, 8:16]
    z = me % 8
    slab = me // 8
    keys1[z] = key_tile.astype(BF16)
    k_copies = []
    for j in range(1, 8):
        h = slab * 8 + (z + j) % 8
        k_copies.append(remote(keys1.at[z], keys1.at[z], k_send.at[0, j], k_recv.at[0, j], (h * 2 + core, mp)))
    for copy in k_copies:
        copy.start()
    for j in range(1, 8):
        bytes_of(keys1.at[(z + 8 - j) % 8], k_recv.at[0, j])
    keys2[slab] = jnp.sum(keys1[...].astype(F32).reshape(2, 4, 16, 128), axis=1).astype(BF16)
    k_copies2 = []
    for j in range(1, 8):
        h = (me + 8 * j) % CHIPS
        k_copies2.append(
            remote(keys2.at[slab], keys2.at[slab], k_send.at[1, j], k_recv.at[1, j], (h * 2 + core, mp))
        )
    for copy in k_copies2:
        copy.start()
    for j in range(1, 8):
        bytes_of(keys2.at[(slab + 8 - j) % 8], k_recv.at[1, j])
    every = keys2[...].reshape(256, 128)
    score = (nt(unit, every) / DIVISOR)[0:8]
    score_out[...] = score[0:2]
    lane = lax.broadcasted_iota(jnp.int32, (8, 256), 1)
    row = lax.broadcasted_iota(jnp.int32, (8, 256), 0)
    matched = jnp.sum(jnp.where(lane == 2 * dp + row, score, 0.0), axis=1, keepdims=True)
    mass_all = jnp.sum(jnp.exp(score), axis=1, keepdims=True) + queue[:, 0:1]
    losses = jnp.broadcast_to(jnp.log(mass_all) - matched, (8, 128))
    lane8 = lax.broadcasted_iota(jnp.int32, (8, 128), 1)
    loss_out[...] = jnp.sum(jnp.where(row8 == lane8, losses, 0.0), axis=0, keepdims=True)[:, 0:2]

    write.wait()
    for copy in rs + sent + sent_stats + ag + halos + e_copies + k_copies + k_copies2:
        copy.wait_send()
    for slot, (src, out) in enumerate(((field, out1), (mid, out2))):

        @pl.when(holder)
        def _():
            bytes_of(src.at[pl.ds(0, BACK - 1)], hop_send.at[slot])
            bytes_of(out.at[pl.ds(0, CHIPS - 1)], out_send.at[slot])

        @pl.when(jnp.logical_not(holder))
        def _():
            bytes_of(src, hop_send.at[slot])


def on_device(
    images,
    permutation,
    inverse,
    reduce_weight,
    reduce_gain,
    reduce_shift,
    spatial_weight,
    spatial_gain,
    spatial_shift,
    expand_weight,
    expand_gain,
    expand_shift,
    projection,
    queries,
    dictionary_bank,
):
    cw = jnp.transpose(spatial_weight, (2, 3, 0, 1))
    rows = [
        v.reshape(1, -1)
        for v in (reduce_gain, reduce_shift, spatial_gain, spatial_shift, expand_gain, expand_shift)
    ]

    vmem = pl.BlockSpec(memory_space=pltpu.VMEM)
    smem = pl.BlockSpec(memory_space=pltpu.SMEM)
    dma = pltpu.SemaphoreType.DMA
    feat, score, loss = pl.pallas_call(
        kernel,
        out_shape=(
            jax.ShapeDtypeStruct((128, PIXELS), BF16),
            jax.ShapeDtypeStruct((2, 256), F32),
            jax.ShapeDtypeStruct((1, 2), F32),
        ),
        in_specs=[smem, smem, pl.BlockSpec(memory_space=pl.ANY)] + [vmem] * 12,
        out_specs=(pl.BlockSpec(memory_space=pl.ANY), vmem, vmem),
        scratch_shapes=[
            pltpu.VMEM((128, PIXELS), BF16),
            pltpu.VMEM((128, PIXELS), BF16),
            pltpu.VMEM((4 * QUARTER, 16, 128), BF16),
            pltpu.VMEM((QUARTER, 16, 128), BF16),
            pltpu.VMEM((QUARTER, 16, 128), BF16),
            pltpu.VMEM((A_TILES, 16, 128), BF16),
            pltpu.VMEM((B_TILES, 16, 128), BF16),
            pltpu.VMEM((A_TILES, 16, 128), BF16),
            pltpu.VMEM((B_TILES, 16, 128), BF16),
            pltpu.VMEM((4, 3, 16, 384), BF16),
            pltpu.VMEM((4, 64, 128), BF16),
            pltpu.VMEM((4, 8, 128), F32),
            pltpu.VMEM((BACK, 16, 128), BF16),
            pltpu.VMEM((CHIPS, 2, 2, 16, 128), BF16),
            pltpu.VMEM((CHIPS, 16, 128), BF16),
            pltpu.VMEM((BACK, 16, 128), BF16),
            pltpu.VMEM((4, 16, 128), F32),
            pltpu.VMEM((4, 16, 128), F32),
            pltpu.VMEM((4, 16, 128), F32),
            pltpu.VMEM((4, 16, 128), F32),
            pltpu.VMEM((BACK, 16, 128), BF16),
            pltpu.VMEM((CHIPS, 2, 2, 16, 128), BF16),
            pltpu.VMEM((CHIPS, 16, 128), BF16),
            pltpu.VMEM((BACK, 16, 128), BF16),
            pltpu.VMEM((4 * QUARTER, 16, 128), BF16),
            pltpu.VMEM((2, 4, 16, 128), F32),
            pltpu.VMEM((8, 16, 128), BF16),
            pltpu.VMEM((8, 2, 16, 128), BF16),
            pltpu.VMEM((4, 16, 128), BF16),
            pltpu.VMEM((4, 16, 128), BF16),
            dma,
            dma,
            dma((7,)),
            dma((7,)),
            dma((3, 3)),
            dma((3, 3)),
            dma((3, 3)),
            dma((3, 3)),
            dma((2,)),
            dma((2, 8)),
            dma((2,)),
            dma((2, 3)),
            dma((2,)),
            dma((2,)),
            dma((2, 8)),
            dma((2, 8)),
            dma((6,)),
            dma((6,)),
            dma((8,)),
            dma((8,)),
            dma((2, 8)),
            dma((2, 8)),
        ],
        compiler_params=pltpu.CompilerParams(
            collective_id=0, has_side_effects=True, vmem_limit_bytes=63 * 1024 * 1024
        ),
        cost_estimate=pl.CostEstimate(
            flops=2 * 3136 * 128 * 128 * 4, bytes_accessed=2 * 128 * 3136 * 2, transcendentals=0
        ),
    )(
        permutation,
        inverse,
        images.reshape(128, PIXELS),
        reduce_weight,
        cw,
        expand_weight,
        *rows,
        projection,
        queries,
        dictionary_bank,
    )
    return feat.reshape(images.shape), score, loss.reshape(2)


def solution(mesh):
    placed = (
        P("dp", "mp", None),
        P(),
        P(),
        P(None, "mp"),
        P("mp"),
        P("mp"),
        P("mp", None, None, None),
        P("mp"),
        P("mp"),
        P("mp", None),
        P("mp"),
        P("mp"),
        P("mp", None),
        P("dp", None),
        P("mp", None),
    )
    return jax.shard_map(
        on_device,
        mesh=mesh,
        in_specs=placed,
        out_specs=(P("dp", "mp", None), P("dp", None), P("dp")),
        check_vma=False,
    )
```

```python
import jax
import jax.numpy as jnp
from jax import lax
from jax.experimental import pallas as pl
from jax.experimental.pallas import tpu as pltpu
from jax.sharding import PartitionSpec as P

MESH = pl.DeviceIdType.MESH
F32 = jnp.float32
BF16 = jnp.bfloat16

SIDE = 56
PIXELS = SIDE * SIDE
COLS = 64
CHIPS = 64
LINES = SIDE // 4
QUARTER = PIXELS // 4 // 16
A_TILES = 25
B_TILES = QUARTER - A_TILES
B_EARLY = 8
BACK = QUARTER + 1
STAT_CHIP = CHIPS - 1
COUNT = 2.0 * (PIXELS // 4)
DIVISOR = 0.2


def nt(a, b):
    return lax.dot_general(a, b, (((1,), (1,)), ((), ())), preferred_element_type=F32)


def tn(a, b):
    return lax.dot_general(a, b, (((0,), (1,)), ((), ())), preferred_element_type=F32)


def remote(src, dst, send, recv, device):
    return pltpu.make_async_remote_copy(
        src_ref=src,
        dst_ref=dst,
        send_sem=send,
        recv_sem=recv,
        device_id=device,
        device_id_type=MESH,
    )


def bytes_of(ref, sem):
    pltpu.make_async_copy(ref, ref, sem).wait()


def kernel(
    perm,
    inv,
    img_hbm,
    rw,
    cw,
    we,
    rg,
    rsh,
    sg,
    ssh,
    eg,
    esh,
    proj,
    queries,
    bank,
    feat_hbm,
    score_out,
    loss_out,
    img,
    feat,
    part,
    from_left,
    from_right,
    via_left,
    via_right,
    sum_a,
    sum_b,
    conv_w,
    exp_w,
    vecs,
    field,
    hold1,
    out1,
    group,
    stat1,
    stat2,
    stat3s,
    stat3,
    mid,
    hold2,
    out2,
    home,
    second_all,
    emb,
    keys1,
    keys2,
    halo_top,
    halo_bottom,
    img_sem,
    feat_sem,
    rs_send,
    rs_recv,
    w_send,
    w_recv,
    s_send,
    s_recv,
    hop_send,
    hop_recv,
    out_send,
    out_recv,
    halo_send,
    halo_recv,
    pair_send,
    pair_recv,
    ag_send,
    ag_recv,
    e_send,
    e_recv,
    k_send,
    k_recv,
):
    dp = lax.axis_index("dp")
    mp = lax.axis_index("mp")
    me = dp // 2
    core = dp % 2
    other = dp + 1 - 2 * core
    right = (mp + 1) % 4
    left = (mp + 3) % 4
    far = (mp + 2) % 4

    fetch = pltpu.make_async_copy(img_hbm, img, img_sem)
    fetch.start()

    barrier = pltpu.get_barrier_semaphore()

    def greet(i, carry):
        for u in range(7):
            h = (me + 1 + 7 * i + u) % CHIPS
            pl.semaphore_signal(barrier, inc=1, device_id=(h * 2 + core, mp), device_id_type=MESH)
        return carry

    for j in range(1, 4):
        pl.semaphore_signal(barrier, inc=1, device_id=(dp, (mp + j) % 4), device_id_type=MESH)
    for j in range(4):
        pl.semaphore_signal(barrier, inc=1, device_id=(other, (mp + j) % 4), device_id_type=MESH)
    lax.fori_loop(0, 9, greet, 0)

    row128 = lax.broadcasted_iota(jnp.int32, (128, 384), 0) // 64
    lane128 = (lax.broadcasted_iota(jnp.int32, (128, 384), 1) // 64) % 2
    same = row128 == lane128
    eye_block = same[:, 0:128]

    def doubled(w):
        w = w.astype(F32)
        return jnp.concatenate([w, w], axis=1)

    def diagonal(w):
        return jnp.where(eye_block, jnp.concatenate([w, w], axis=0), 0.0).astype(BF16)

    rw_block = diagonal(doubled(rw[...]))
    fetch.wait()

    for k in range(5):
        n = 40 if k < 4 else 36
        block = tn(img[:, 640 * k : 640 * k + 16 * n], rw_block)
        part[40 * k : 40 * k + n] = block.astype(BF16).reshape(n, 16, 128)

    pl.semaphore_wait(barrier, CHIPS - 1 + 7)

    def a_part(q):
        return part.at[pl.ds(QUARTER * q, A_TILES)]

    def b_part(q):
        return part.at[pl.ds(QUARTER * q + A_TILES, B_TILES)]

    to_r = (dp, right)
    to_l = (dp, left)
    left_a = from_left.at[pl.ds(0, A_TILES)]
    left_b = from_left.at[pl.ds(A_TILES, B_TILES)]
    right_a = from_right.at[pl.ds(0, A_TILES)]
    right_b = from_right.at[pl.ds(A_TILES, B_TILES)]
    b_first = part.at[pl.ds(QUARTER * right + A_TILES, B_EARLY)]
    b_later = part.at[pl.ds(QUARTER * right + A_TILES + B_EARLY, B_TILES - B_EARLY)]
    left_b_first = from_left.at[pl.ds(A_TILES, B_EARLY)]
    left_b_later = from_left.at[pl.ds(A_TILES + B_EARLY, B_TILES - B_EARLY)]
    rs = [
        remote(a_part(far), via_left, rs_send.at[0], rs_recv.at[0], to_r),
        remote(b_part(far), via_right, rs_send.at[3], rs_recv.at[3], to_l),
        remote(b_first, left_b_first, rs_send.at[2], rs_recv.at[2], to_r),
        remote(a_part(left), right_a, rs_send.at[1], rs_recv.at[1], to_l),
        remote(sum_a, left_a, rs_send.at[4], rs_recv.at[4], to_r),
        remote(b_later, left_b_later, rs_send.at[6], rs_recv.at[6], to_r),
        remote(sum_b, right_b, rs_send.at[5], rs_recv.at[5], to_l),
    ]
    for copy in rs[:4]:
        copy.start()

    vin = jnp.concatenate([rg[...], rsh[...], sg[...], ssh[...], eg[...], esh[...]], axis=1)
    we_wide = doubled(we[...])
    we_block = diagonal(we_wide)
    v_row = lax.broadcasted_iota(jnp.int32, (8, 192), 0)
    v_lane = lax.broadcasted_iota(jnp.int32, (8, 192), 1)
    v_in = jnp.where(v_lane // 16 == v_row, jnp.broadcast_to(vin, (8, 192)), 0.0)
    v_in = jnp.where(v_row < 4, v_in, 0.0)
    p_row = lax.broadcasted_iota(jnp.int32, (192, 128), 0)
    p_lane = lax.broadcasted_iota(jnp.int32, (192, 128), 1)
    v_place = jnp.where(p_row % 16 + 16 * mp == p_lane % 64, 1.0, 0.0)
    vec = jnp.dot(v_in, v_place, precision=lax.Precision.HIGHEST, preferred_element_type=F32)
    c_row = lax.broadcasted_iota(jnp.int32, (128, 192), 0) % 64
    c_lane = lax.broadcasted_iota(jnp.int32, (128, 192), 1)
    v_all = jnp.broadcast_to(vin, (128, 192))
    gain_c = jnp.sum(jnp.where(c_lane == c_row + 64, v_all, 0.0), axis=1, keepdims=True)
    shift_c = jnp.sum(jnp.where(c_lane == c_row + 128, v_all, 0.0), axis=1, keepdims=True)
    for dy in range(3):
        conv_w[mp, dy] = jnp.concatenate([doubled(cw[dy, dx]) for dx in range(3)], axis=1).astype(BF16)
    exp_w[mp] = we_wide.astype(BF16)
    vecs[mp] = vec

    def share(buf, n):
        copies = [
            remote(buf.at[mp], buf.at[mp], w_send.at[n, j - 1], w_recv.at[n, j - 1], (dp, (mp + j) % 4))
            for j in range(1, 4)
        ]
        for copy in copies:
            copy.start()
        return copies

    def shared(buf, copies, n):
        for j in range(1, 4):
            src = buf.at[(mp + 4 - j) % 4]
            bytes_of(src, w_recv.at[n, j - 1])

    sent = []

    q_row = lax.broadcasted_iota(jnp.int32, (16, 128), 0)
    q_all = jnp.where(q_row == 0, queries[0:1, :], jnp.where(q_row == 1, queries[1:2, :], 0.0))
    unit = (q_all * lax.rsqrt(jnp.sum(q_all * q_all, axis=1, keepdims=True) + 1e-06)).astype(BF16)
    stored = nt(unit, bank[...]) / DIVISOR
    mass = jnp.broadcast_to(jnp.sum(jnp.exp(stored), axis=1, keepdims=True), (16, 128))

    rs[0].wait_recv()
    own = part[pl.ds(QUARTER * right, A_TILES)].astype(F32)
    sum_a[...] = (own + via_left[...].astype(F32)).astype(BF16)
    rs[4].start()
    rs[5].start()
    rs[1].wait_recv()
    own = part[pl.ds(QUARTER * left + A_TILES, B_TILES)].astype(F32)
    sum_b[...] = (own + via_right[...].astype(F32)).astype(BF16)
    rs[6].start()


    low = lax.broadcasted_iota(jnp.int32, (16, 128), 1) < 64
    pair = me // 2
    holds_a = jnp.logical_and(me % 2 == 0, pair < A_TILES)
    holds_b = jnp.logical_and(me % 2 == 1, pair < B_TILES)
    holds_s = me == STAT_CHIP
    holds_data = jnp.logical_or(holds_a, holds_b)
    holder = jnp.logical_or(holds_data, holds_s)
    held = jnp.where(holds_s, QUARTER, jnp.where(holds_a, pair, pair + A_TILES))
    held_part = jnp.where(holds_s, 2, jnp.where(holds_a, 0, 1))

    def send_tile(src, t, hold, h, slot):
        remote(
            src.at[t],
            hold.at[me, core, 0],
            hop_send.at[slot],
            hop_recv.at[slot, me // 8],
            (h * 2 + core, mp),
        ).start()

    def spread(src, hold, odd, slot):
        n = B_TILES if odd else A_TILES

        def step(i, carry):
            for u in range(8):
                t = (pair + 8 * i + u) % (CHIPS // 2)
                h = 2 * t + odd

                @pl.when(jnp.logical_and(h != me, t < n))
                def _():
                    send_tile(src, t + odd * A_TILES, hold, h, slot)

            return carry

        lax.fori_loop(0, 4, step, 0)

        @pl.when(holds_b if odd else holds_a)
        def _():
            hold[me, core, 0] = src[pair + odd * A_TILES]

    def spread_stats(src, hold, slot):
        @pl.when(me != STAT_CHIP)
        def _():
            send_tile(src, QUARTER, hold, STAT_CHIP, slot)

        @pl.when(holds_s)
        def _():
            hold[STAT_CHIP, core, 0] = src[QUARTER]

    def receive(hold, slot, holds):
        def turn(side, g):
            at = pl.ds(8 * g, 8)
            x = hold[at, side, 0].reshape(128, 128).astype(F32)
            hold[at, side, 1] = pltpu.roll(x, 64, 1).astype(BF16).reshape(8, 16, 128)

        def swapping(g):
            ref = hold.at[pl.ds(8 * g, 8), core, 0]
            return remote(ref, ref, pair_send.at[slot, g], pair_recv.at[slot, g], (other, mp))

        def take(i, carry):
            g = (me // 8 + 8 - i) % 8
            bytes_of(hold.at[pl.ds(8 * g, 8), core, 0], hop_recv.at[slot, g])
            swapping(g).start()
            turn(core, g)
            return carry

        def take_other(i, carry):
            g = (me // 8 + 16 - i) % 8
            bytes_of(hold.at[pl.ds(8 * g, 8), 1 - core, 0], pair_recv.at[slot, g])
            turn(1 - core, g)
            return carry

        def swapped(i, carry):
            swapping(i).wait_send()
            return carry

        @pl.when(holds)
        def _():
            lax.fori_loop(1, 8, take, 0)
            g = me // 8
            bytes_of(hold.at[pl.ds(8 * g, 7), core, 0], hop_recv.at[slot, g])
            swapping(g).start()
            turn(core, g)
            lax.fori_loop(1, 9, take_other, 0)
            lax.fori_loop(0, 8, swapped, 0)

    def deal(hold, order, out, dst, slot, holds, tile, part_of):
        def pick(t):
            at = 4 * t + 2 * core
            i0 = order[at]
            i1 = order[at + 1]
            x0 = hold[i0 >> 2, (i0 >> 1) & 1, i0 & 1]
            x1 = hold[i1 >> 2, (i1 >> 1) & 1, 1 - (i1 & 1)]
            return jnp.where(low, x0, x1)

        @pl.when(holds)
        def _():
            def step(i, carry):
                ts = [(me + 1 + 9 * i + u) % CHIPS for u in range(9)]
                values = [pick(t) for t in ts]
                for t, value in zip(ts, values):
                    out[t] = value
                for t in ts:
                    remote(
                        out.at[t],
                        dst.at[tile],
                        out_send.at[slot],
                        out_recv.at[slot, part_of],
                        (t * 2 + core, mp),
                    ).start()
                return carry

            lax.fori_loop(0, 7, step, 0)
            dst[tile] = pick(me)

    def arrived(dst, slot, part_of):
        start, n, holds = ((0, A_TILES, holds_a), (A_TILES, B_TILES, holds_b), (QUARTER, 1, holds_s))[part_of]

        @pl.when(jnp.logical_not(holds))
        def _():
            bytes_of(dst.at[pl.ds(start, n)], out_recv.at[slot, part_of])

        if n > 1:

            @pl.when(holds)
            def _():
                bytes_of(dst.at[pl.ds(start, n - 1)], out_recv.at[slot, part_of])

    rs[4].wait_recv()
    rs[3].wait_recv()
    total = part[pl.ds(QUARTER * mp, A_TILES)].astype(F32)
    total = total + left_a[...].astype(F32) + right_a[...].astype(F32)
    field[0:A_TILES] = total.astype(BF16)
    spread(field, hold1, 0, 0)

    for copy in (rs[2], rs[5], rs[6]):
        copy.wait_recv()
    total = part[pl.ds(QUARTER * mp + A_TILES, B_TILES)].astype(F32)
    total = total + left_b[...].astype(F32) + right_b[...].astype(F32)
    field[A_TILES:QUARTER] = total.astype(BF16)
    spread(field, hold1, 1, 0)

    def both(x):
        x = jnp.broadcast_to(x, (8, 128))
        return x + pltpu.roll(x, 64, 1)

    def offer(buf, tile, n):
        buf[mp] = tile
        copies = [
            remote(buf.at[mp], buf.at[mp], s_send.at[n, j - 1], s_recv.at[n, j - 1], (dp, (mp + j) % 4))
            for j in range(1, 4)
        ]
        for copy in copies:
            copy.start()
        return copies

    def collect(buf, n):
        for j in range(1, 4):
            bytes_of(buf.at[(mp + 4 - j) % 4], s_recv.at[n, j - 1])

    def local_stats(x):
        mean = both(jnp.sum(x, axis=0, keepdims=True)) / COUNT
        dev = x - mean[0:1]
        square = both(jnp.sum(dev * dev, axis=0, keepdims=True))
        return jnp.concatenate([mean, square], axis=0)

    def whole_stats(buf, count):
        means = [buf[q, 0:1, :] for q in range(4)]
        mean = (means[0] + means[1] + means[2] + means[3]) * 0.25
        square = jnp.zeros((1, 128), F32)
        for q in range(4):
            off = means[q] - mean
            square = square + buf[q, 8:9, :] + count * (off * off)
        return mean, square / (4.0 * count)

    def pieces(v):
        a = v.astype(BF16).astype(F32)
        b = (v - a).astype(BF16).astype(F32)
        return [a, b, v - a - b]

    x = field[0:QUARTER].reshape(16 * QUARTER, 128).astype(F32)
    half_count = COUNT / 2.0
    mean = jnp.sum(x, axis=0, keepdims=True) / half_count
    dev = x - mean
    square = jnp.sum(dev * dev, axis=0, keepdims=True)
    tile = jnp.concatenate([jnp.broadcast_to(mean, (8, 128)), jnp.broadcast_to(square, (8, 128))], axis=0)
    sent_stats = offer(stat1, tile, 0)
    sent += share(conv_w, 0)
    sent += share(exp_w, 1)
    sent += share(vecs, 2)
    receive(hold1, 0, holds_data)
    collect(stat1, 0)
    mean, var = whole_stats(stat1, half_count)

    def stat_tile(values):
        tile = jnp.zeros((16, 128), F32)
        for r, v in enumerate(values):
            tile = jnp.where(q_row == r, v, tile)
        return tile.astype(BF16)

    field[QUARTER] = stat_tile(pieces(mean) + pieces(var))
    spread_stats(field, hold1, 0)
    receive(hold1, 0, holds_s)

    deal(hold1, perm, out1, group, 0, holder, held, held_part)
    for n, buf in enumerate((conv_w, exp_w, vecs)):
        shared(buf, sent, n)
    conv_blocks = []
    for dy in range(3):
        w = jnp.concatenate([conv_w[q, dy] for q in range(4)] * 2, axis=0).astype(F32)
        conv_blocks.append(jnp.where(same, w, 0.0).astype(BF16))
    vec_all = vecs[0] + vecs[1] + vecs[2] + vecs[3]
    arrived(group, 0, 0)
    arrived(group, 0, 1)
    halos = [
        remote(group.at[pl.ds(0, 4)], halo_bottom, halo_send.at[0], halo_recv.at[0], to_l),
        remote(group.at[pl.ds(QUARTER - 4, 4)], halo_top, halo_send.at[1], halo_recv.at[1], to_r),
    ]
    for copy in halos:
        copy.start()
    arrived(group, 0, 2)


    marks = group[QUARTER].astype(F32)
    mean_i = marks[0:1] + marks[1:2] + marks[2:3]
    var_i = marks[3:4] + marks[4:5] + marks[5:6]
    mean = (both(mean_i) * 0.5)[0:1]
    off = mean_i - mean
    var = (both(var_i + off * off) * 0.5)[0:1]
    scale = lax.rsqrt(var + 1e-05)

    def norm1(tiles):
        x = tiles.reshape(-1, 128).astype(F32)
        return jnp.maximum((x - mean) * scale * vec_all[0:1] + vec_all[1:2], 0.0)

    inner = norm1(group[0:QUARTER]).reshape(LINES, SIDE, 128)
    for copy in halos:
        copy.wait_recv()
    top = norm1(halo_top[...])[8:64]
    bottom = norm1(halo_bottom[...])[0:SIDE]
    top = jnp.where(jnp.full((SIDE, 128), mp, jnp.int32) == 0, 0.0, top).reshape(1, SIDE, 128)
    bottom = jnp.where(jnp.full((SIDE, 128), mp, jnp.int32) == 3, 0.0, bottom).reshape(1, SIDE, 128)
    first = jnp.concatenate([top, inner, bottom], axis=0)
    first = jnp.concatenate([first, jnp.zeros((LINES + 2, COLS - SIDE, 128), F32)], axis=1)
    first = first.reshape((LINES + 2) * COLS, 128)

    wide = jnp.concatenate(
        [
            pltpu.roll(first, 1, 0).astype(BF16),
            first.astype(BF16),
            pltpu.roll(first, (LINES + 2) * COLS - 1, 0).astype(BF16),
        ],
        axis=1,
    )
    n_out = LINES * COLS
    spatial = nt(wide[0:n_out], conv_blocks[0])
    spatial = spatial + nt(wide[COLS : COLS + n_out], conv_blocks[1])
    spatial = spatial + nt(wide[2 * COLS : 2 * COLS + n_out], conv_blocks[2])
    spatial = spatial.reshape(LINES, COLS, 128)[:, :SIDE, :].reshape(16 * QUARTER, 128)

    sent_stats += offer(stat2, local_stats(spatial), 1)
    collect(stat2, 1)
    mean, var = whole_stats(stat2, COUNT)
    second = jnp.maximum((spatial - mean) * lax.rsqrt(var + 1e-05) * vec_all[2:3] + vec_all[3:4], 0.0).astype(BF16)
    mid[0:QUARTER] = second.reshape(QUARTER, 16, 128)
    spread(mid, hold2, 0, 1)
    spread(mid, hold2, 1, 1)

    copies3 = []
    for q in range(4):
        stat3s[q] = local_stats(nt(second, diagonal(exp_w[q].astype(F32))))
    for j in range(1, 4):
        q = (mp + j) % 4
        copy = remote(stat3s.at[q], stat3.at[mp], s_send.at[2, j - 1], s_recv.at[2, j - 1], (dp, q))
        copy.start()
        copies3.append(copy)
    stat3[mp] = stat3s[mp]
    sent_stats += copies3
    receive(hold2, 1, holds_data)
    collect(stat3, 2)
    mean, var = whole_stats(stat3, COUNT)
    mid[QUARTER] = stat_tile(pieces(mean) + pieces(lax.rsqrt(var + 1e-05)))
    spread_stats(mid, hold2, 1)
    receive(hold2, 1, holds_s)
    deal(hold2, inv, out2, home, 1, holder, held, held_part)

    def a_of(q):
        return second_all.at[pl.ds(QUARTER * q, A_TILES)]

    def b_of(q):
        return second_all.at[pl.ds(QUARTER * q + A_TILES, B_TILES)]

    ag = [
        remote(a_of(mp), a_of(mp), ag_send.at[0], ag_recv.at[0], to_r),
        remote(a_of(mp), a_of(mp), ag_send.at[1], ag_recv.at[1], to_l),
        remote(b_of(mp), b_of(mp), ag_send.at[2], ag_recv.at[2], to_l),
        remote(b_of(mp), b_of(mp), ag_send.at[3], ag_recv.at[3], to_r),
        remote(a_of(left), a_of(left), ag_send.at[4], ag_recv.at[4], to_r),
        remote(b_of(right), b_of(right), ag_send.at[5], ag_recv.at[5], to_l),
    ]
    arrived(home, 1, 0)
    second_all[pl.ds(QUARTER * mp, A_TILES)] = home[0:A_TILES]
    ag[0].start()
    arrived(home, 1, 1)
    second_all[pl.ds(QUARTER * mp + A_TILES, B_TILES)] = home[A_TILES:QUARTER]
    ag[2].start()
    ag[3].start()
    ag[1].start()
    bytes_of(a_of(left), ag_recv.at[0])
    ag[4].start()
    bytes_of(b_of(right), ag_recv.at[2])
    ag[5].start()
    arrived(home, 1, 2)

    identity = jnp.where(
        lax.broadcasted_iota(jnp.int32, (128, 128), 0) == lax.broadcasted_iota(jnp.int32, (128, 128), 1),
        1.0,
        0.0,
    ).astype(BF16)
    columns = nt(identity, home[QUARTER])
    mean_c = columns[:, 0:1] + columns[:, 1:2] + columns[:, 2:3]
    scale_c = columns[:, 3:4] + columns[:, 4:5] + columns[:, 5:6]

    def expand(block, lanes):
        v = nt(we_block, block)
        third = ((v - mean_c) * scale_c * gain_c + shift_c).astype(BF16).astype(F32)
        f = jnp.maximum(third + img[:, lanes].astype(F32), 0.0).astype(BF16)
        feat[:, lanes] = f
        return f.astype(F32)

    def expand_at(i, pooled):
        j = ((QUARTER * far + QUARTER - 1) // 32 + 1 + i) % 6
        block = second_all[pl.ds(32 * j, 32)].reshape(512, 128)
        f = expand(block, pl.ds(pl.multiple_of(512 * j, 512), 512))
        return pooled + (f[:, 0:128] + f[:, 128:256] + f[:, 256:384] + f[:, 384:512])

    bytes_of(a_of(right), ag_recv.at[1])
    bytes_of(b_of(left), ag_recv.at[3])
    pooled = jnp.zeros((128, 128), F32)
    for i in range(3):
        pooled = expand_at(i, pooled)
    bytes_of(a_of(far), ag_recv.at[4])
    bytes_of(b_of(far), ag_recv.at[5])
    for i in range(3, 6):
        pooled = expand_at(i, pooled)
    rest = expand(second_all[192:196].reshape(64, 128), slice(3072, 3136))
    write = pltpu.make_async_copy(feat, feat_hbm, feat_sem)
    write.start()
    pooled = jnp.sum(pooled, axis=1, keepdims=True) + jnp.sum(rest, axis=1, keepdims=True)
    pooled = pooled / float(PIXELS)

    proj2 = jnp.concatenate([proj[...], proj[...]], axis=0).astype(F32)
    terms = pooled * proj2
    e0 = jnp.sum(terms[0:64], axis=0, keepdims=True)
    e1 = jnp.sum(terms[64:128], axis=0, keepdims=True)
    row8 = lax.broadcasted_iota(jnp.int32, (8, 128), 0)
    top = jnp.where(row8 == 0, e0, jnp.where(row8 == 1, e1, 0.0))
    emb[core, mp] = jnp.concatenate([top, mass[0:8]], axis=0)
    mine = emb.at[core, mp]
    e_copies = []
    for j in range(1, 4):
        e_copies.append(remote(mine, mine, e_send.at[j], e_recv.at[j], (dp, (mp + j) % 4)))
    for j in range(4):
        e_copies.append(remote(mine, mine, e_send.at[4 + j], e_recv.at[4 + j], (other, (mp + j) % 4)))
    for copy in e_copies:
        copy.start()
    for j in range(1, 4):
        bytes_of(emb.at[core, (mp + 4 - j) % 4], e_recv.at[j])
    for j in range(4):
        bytes_of(emb.at[1 - core, (mp + 4 - j) % 4], e_recv.at[4 + j])

    key_tile = jnp.zeros((16, 128), F32)
    for cc in range(2):
        e = emb[cc, 0, 0:8] + emb[cc, 1, 0:8] + emb[cc, 2, 0:8] + emb[cc, 3, 0:8]
        key = e * lax.rsqrt(jnp.sum(e * e, axis=1, keepdims=True) + 1e-06)
        for b in range(2):
            here = q_row == 4 * (me % 4) + 2 * cc + b
            key_tile = jnp.where(here, key[b : b + 1], key_tile)
    queue = emb[core, 0, 8:16] + emb[core, 1, 8:16] + emb[core, 2, 8:16] + emb[core, 3, 8:16]
    z = me % 8
    slab = me // 8
    keys1[z] = key_tile.astype(BF16)
    k_copies = []
    for j in range(1, 8):
        h = slab * 8 + (z + j) % 8
        k_copies.append(remote(keys1.at[z], keys1.at[z], k_send.at[0, j], k_recv.at[0, j], (h * 2 + core, mp)))
    for copy in k_copies:
        copy.start()
    for j in range(1, 8):
        bytes_of(keys1.at[(z + 8 - j) % 8], k_recv.at[0, j])
    keys2[slab] = jnp.sum(keys1[...].astype(F32).reshape(2, 4, 16, 128), axis=1).astype(BF16)
    k_copies2 = []
    for j in range(1, 8):
        h = (me + 8 * j) % CHIPS
        k_copies2.append(
            remote(keys2.at[slab], keys2.at[slab], k_send.at[1, j], k_recv.at[1, j], (h * 2 + core, mp))
        )
    for copy in k_copies2:
        copy.start()
    for j in range(1, 8):
        bytes_of(keys2.at[(slab + 8 - j) % 8], k_recv.at[1, j])
    every = keys2[...].reshape(256, 128)
    score = (nt(unit, every) / DIVISOR)[0:8]
    score_out[...] = score[0:2]
    lane = lax.broadcasted_iota(jnp.int32, (8, 256), 1)
    row = lax.broadcasted_iota(jnp.int32, (8, 256), 0)
    matched = jnp.sum(jnp.where(lane == 2 * dp + row, score, 0.0), axis=1, keepdims=True)
    mass_all = jnp.sum(jnp.exp(score), axis=1, keepdims=True) + queue[:, 0:1]
    losses = jnp.broadcast_to(jnp.log(mass_all) - matched, (8, 128))
    lane8 = lax.broadcasted_iota(jnp.int32, (8, 128), 1)
    loss_out[...] = jnp.sum(jnp.where(row8 == lane8, losses, 0.0), axis=0, keepdims=True)[:, 0:2]

    write.wait()
    for copy in rs + sent + sent_stats + ag + halos + e_copies + k_copies + k_copies2:
        copy.wait_send()
    for slot, (src, out) in enumerate(((field, out1), (mid, out2))):

        @pl.when(holder)
        def _():
            bytes_of(src.at[pl.ds(0, BACK - 1)], hop_send.at[slot])
            bytes_of(out.at[pl.ds(0, CHIPS - 1)], out_send.at[slot])

        @pl.when(jnp.logical_not(holder))
        def _():
            bytes_of(src, hop_send.at[slot])


def on_device(
    images,
    permutation,
    inverse,
    reduce_weight,
    reduce_gain,
    reduce_shift,
    spatial_weight,
    spatial_gain,
    spatial_shift,
    expand_weight,
    expand_gain,
    expand_shift,
    projection,
    queries,
    dictionary_bank,
):
    cw = jnp.transpose(spatial_weight, (2, 3, 0, 1))
    rows = [
        v.reshape(1, -1)
        for v in (reduce_gain, reduce_shift, spatial_gain, spatial_shift, expand_gain, expand_shift)
    ]

    vmem = pl.BlockSpec(memory_space=pltpu.VMEM)
    smem = pl.BlockSpec(memory_space=pltpu.SMEM)
    dma = pltpu.SemaphoreType.DMA
    feat, score, loss = pl.pallas_call(
        kernel,
        out_shape=(
            jax.ShapeDtypeStruct((128, PIXELS), BF16),
            jax.ShapeDtypeStruct((2, 256), F32),
            jax.ShapeDtypeStruct((1, 2), F32),
        ),
        in_specs=[smem, smem, pl.BlockSpec(memory_space=pl.ANY)] + [vmem] * 12,
        out_specs=(pl.BlockSpec(memory_space=pl.ANY), vmem, vmem),
        scratch_shapes=[
            pltpu.VMEM((128, PIXELS), BF16),
            pltpu.VMEM((128, PIXELS), BF16),
            pltpu.VMEM((4 * QUARTER, 16, 128), BF16),
            pltpu.VMEM((QUARTER, 16, 128), BF16),
            pltpu.VMEM((QUARTER, 16, 128), BF16),
            pltpu.VMEM((A_TILES, 16, 128), BF16),
            pltpu.VMEM((B_TILES, 16, 128), BF16),
            pltpu.VMEM((A_TILES, 16, 128), BF16),
            pltpu.VMEM((B_TILES, 16, 128), BF16),
            pltpu.VMEM((4, 3, 16, 384), BF16),
            pltpu.VMEM((4, 64, 128), BF16),
            pltpu.VMEM((4, 8, 128), F32),
            pltpu.VMEM((BACK, 16, 128), BF16),
            pltpu.VMEM((CHIPS, 2, 2, 16, 128), BF16),
            pltpu.VMEM((CHIPS, 16, 128), BF16),
            pltpu.VMEM((BACK, 16, 128), BF16),
            pltpu.VMEM((4, 16, 128), F32),
            pltpu.VMEM((4, 16, 128), F32),
            pltpu.VMEM((4, 16, 128), F32),
            pltpu.VMEM((4, 16, 128), F32),
            pltpu.VMEM((BACK, 16, 128), BF16),
            pltpu.VMEM((CHIPS, 2, 2, 16, 128), BF16),
            pltpu.VMEM((CHIPS, 16, 128), BF16),
            pltpu.VMEM((BACK, 16, 128), BF16),
            pltpu.VMEM((4 * QUARTER, 16, 128), BF16),
            pltpu.VMEM((2, 4, 16, 128), F32),
            pltpu.VMEM((8, 16, 128), BF16),
            pltpu.VMEM((8, 2, 16, 128), BF16),
            pltpu.VMEM((4, 16, 128), BF16),
            pltpu.VMEM((4, 16, 128), BF16),
            dma,
            dma,
            dma((7,)),
            dma((7,)),
            dma((3, 3)),
            dma((3, 3)),
            dma((3, 3)),
            dma((3, 3)),
            dma((2,)),
            dma((2, 8)),
            dma((2,)),
            dma((2, 3)),
            dma((2,)),
            dma((2,)),
            dma((2, 8)),
            dma((2, 8)),
            dma((6,)),
            dma((6,)),
            dma((8,)),
            dma((8,)),
            dma((2, 8)),
            dma((2, 8)),
        ],
        compiler_params=pltpu.CompilerParams(
            collective_id=0, has_side_effects=True, vmem_limit_bytes=63 * 1024 * 1024
        ),
        cost_estimate=pl.CostEstimate(
            flops=2 * 3136 * 128 * 128 * 4, bytes_accessed=2 * 128 * 3136 * 2, transcendentals=0
        ),
    )(
        permutation,
        inverse,
        images.reshape(128, PIXELS),
        reduce_weight,
        cw,
        expand_weight,
        *rows,
        projection,
        queries,
        dictionary_bank,
    )
    return feat.reshape(images.shape), score, loss.reshape(2)


def solution(mesh):
    placed = (
        P("dp", "mp", None),
        P(),
        P(),
        P(None, "mp"),
        P("mp"),
        P("mp"),
        P("mp", None, None, None),
        P("mp"),
        P("mp"),
        P("mp", None),
        P("mp"),
        P("mp"),
        P("mp", None),
        P("dp", None),
        P("mp", None),
    )
    return jax.shard_map(
        on_device,
        mesh=mesh,
        in_specs=placed,
        out_specs=(P("dp", "mp", None), P("dp", None), P("dp")),
        check_vma=False,
    )
```

```python
import jax
import jax.numpy as jnp
from jax import lax
from jax.experimental import pallas as pl
from jax.experimental.pallas import tpu as pltpu
from jax.sharding import PartitionSpec as P

MESH = pl.DeviceIdType.MESH
F32 = jnp.float32
BF16 = jnp.bfloat16

SIDE = 56
PIXELS = SIDE * SIDE
COLS = 64
CHIPS = 64
LINES = SIDE // 4
QUARTER = PIXELS // 4 // 16
A_TILES = 24
B_TILES = QUARTER - A_TILES
B_EARLY = 8
A_PAIRS = 12
DATA_PAIRS = 25
BACK = DATA_PAIRS + 1
COUNT = 2.0 * (PIXELS // 4)
DIVISOR = 0.2


def nt(a, b):
    return lax.dot_general(a, b, (((1,), (1,)), ((), ())), preferred_element_type=F32)


def tn(a, b):
    return lax.dot_general(a, b, (((0,), (1,)), ((), ())), preferred_element_type=F32)


def remote(src, dst, send, recv, device):
    return pltpu.make_async_remote_copy(
        src_ref=src,
        dst_ref=dst,
        send_sem=send,
        recv_sem=recv,
        device_id=device,
        device_id_type=MESH,
    )


def bytes_of(ref, sem):
    pltpu.make_async_copy(ref, ref, sem).wait()


def kernel(
    perm,
    inv,
    img_hbm,
    rw,
    cw,
    we,
    rg,
    rsh,
    sg,
    ssh,
    eg,
    esh,
    proj,
    queries,
    bank,
    feat_hbm,
    score_out,
    loss_out,
    img,
    feat,
    part,
    from_left,
    from_right,
    via_left,
    via_right,
    sum_a,
    sum_b,
    conv_w,
    exp_w,
    vecs,
    field,
    hold1,
    out1,
    group,
    stat1,
    stat2,
    stat3s,
    stat3,
    mid,
    hold2,
    out2,
    home,
    second_all,
    emb,
    keys1,
    keys2,
    halo_top,
    halo_bottom,
    img_sem,
    feat_sem,
    rs_send,
    rs_recv,
    w_send,
    w_recv,
    s_send,
    s_recv,
    hop_send,
    hop_recv,
    out_send,
    out_recv,
    halo_send,
    halo_recv,
    pair_send,
    pair_recv,
    ag_send,
    ag_recv,
    e_send,
    e_recv,
    k_send,
    k_recv,
):
    dp = lax.axis_index("dp")
    mp = lax.axis_index("mp")
    me = dp // 2
    core = dp % 2
    other = dp + 1 - 2 * core
    right = (mp + 1) % 4
    left = (mp + 3) % 4
    far = (mp + 2) % 4

    fetch = pltpu.make_async_copy(img_hbm, img, img_sem)
    fetch.start()

    barrier = pltpu.get_barrier_semaphore()

    def greet(i, carry):
        for u in range(7):
            h = (me + 1 + 7 * i + u) % CHIPS
            pl.semaphore_signal(barrier, inc=1, device_id=(h * 2 + core, mp), device_id_type=MESH)
        return carry

    for j in range(1, 4):
        pl.semaphore_signal(barrier, inc=1, device_id=(dp, (mp + j) % 4), device_id_type=MESH)
    for j in range(4):
        pl.semaphore_signal(barrier, inc=1, device_id=(other, (mp + j) % 4), device_id_type=MESH)
    lax.fori_loop(0, 9, greet, 0)

    row128 = lax.broadcasted_iota(jnp.int32, (128, 384), 0) // 64
    lane128 = (lax.broadcasted_iota(jnp.int32, (128, 384), 1) // 64) % 2
    same = row128 == lane128
    eye_block = same[:, 0:128]

    def doubled(w):
        w = w.astype(F32)
        return jnp.concatenate([w, w], axis=1)

    def diagonal(w):
        return jnp.where(eye_block, jnp.concatenate([w, w], axis=0), 0.0).astype(BF16)

    rw_block = diagonal(doubled(rw[...]))
    fetch.wait()

    for k in range(5):
        n = 40 if k < 4 else 36
        block = tn(img[:, 640 * k : 640 * k + 16 * n], rw_block)
        part[40 * k : 40 * k + n] = block.astype(BF16).reshape(n, 16, 128)

    pl.semaphore_wait(barrier, CHIPS - 1 + 7)

    def a_part(q):
        return part.at[pl.ds(QUARTER * q, A_TILES)]

    def b_part(q):
        return part.at[pl.ds(QUARTER * q + A_TILES, B_TILES)]

    to_r = (dp, right)
    to_l = (dp, left)
    left_a = from_left.at[pl.ds(0, A_TILES)]
    left_b = from_left.at[pl.ds(A_TILES, B_TILES)]
    right_a = from_right.at[pl.ds(0, A_TILES)]
    right_b = from_right.at[pl.ds(A_TILES, B_TILES)]
    b_first = part.at[pl.ds(QUARTER * right + A_TILES, B_EARLY)]
    b_later = part.at[pl.ds(QUARTER * right + A_TILES + B_EARLY, B_TILES - B_EARLY)]
    left_b_first = from_left.at[pl.ds(A_TILES, B_EARLY)]
    left_b_later = from_left.at[pl.ds(A_TILES + B_EARLY, B_TILES - B_EARLY)]
    rs = [
        remote(a_part(far), via_left, rs_send.at[0], rs_recv.at[0], to_r),
        remote(b_part(far), via_right, rs_send.at[3], rs_recv.at[3], to_l),
        remote(b_first, left_b_first, rs_send.at[2], rs_recv.at[2], to_r),
        remote(a_part(left), right_a, rs_send.at[1], rs_recv.at[1], to_l),
        remote(sum_a, left_a, rs_send.at[4], rs_recv.at[4], to_r),
        remote(b_later, left_b_later, rs_send.at[6], rs_recv.at[6], to_r),
        remote(sum_b, right_b, rs_send.at[5], rs_recv.at[5], to_l),
    ]
    for copy in rs[:4]:
        copy.start()

    vin = jnp.concatenate([rg[...], rsh[...], sg[...], ssh[...], eg[...], esh[...]], axis=1)
    we_wide = doubled(we[...])
    we_block = diagonal(we_wide)
    v_row = lax.broadcasted_iota(jnp.int32, (8, 192), 0)
    v_lane = lax.broadcasted_iota(jnp.int32, (8, 192), 1)
    v_in = jnp.where(v_lane // 16 == v_row, jnp.broadcast_to(vin, (8, 192)), 0.0)
    v_in = jnp.where(v_row < 4, v_in, 0.0)
    p_row = lax.broadcasted_iota(jnp.int32, (192, 128), 0)
    p_lane = lax.broadcasted_iota(jnp.int32, (192, 128), 1)
    v_place = jnp.where(p_row % 16 + 16 * mp == p_lane % 64, 1.0, 0.0)
    vec = jnp.dot(v_in, v_place, precision=lax.Precision.HIGHEST, preferred_element_type=F32)
    c_row = lax.broadcasted_iota(jnp.int32, (128, 192), 0) % 64
    c_lane = lax.broadcasted_iota(jnp.int32, (128, 192), 1)
    v_all = jnp.broadcast_to(vin, (128, 192))
    gain_c = jnp.sum(jnp.where(c_lane == c_row + 64, v_all, 0.0), axis=1, keepdims=True)
    shift_c = jnp.sum(jnp.where(c_lane == c_row + 128, v_all, 0.0), axis=1, keepdims=True)
    for dy in range(3):
        conv_w[mp, dy] = jnp.concatenate([doubled(cw[dy, dx]) for dx in range(3)], axis=1).astype(BF16)
    exp_w[mp] = we_wide.astype(BF16)
    vecs[mp] = vec

    def share(buf, n):
        copies = [
            remote(buf.at[mp], buf.at[mp], w_send.at[n, j - 1], w_recv.at[n, j - 1], (dp, (mp + j) % 4))
            for j in range(1, 4)
        ]
        for copy in copies:
            copy.start()
        return copies

    def shared(buf, copies, n):
        for j in range(1, 4):
            src = buf.at[(mp + 4 - j) % 4]
            bytes_of(src, w_recv.at[n, j - 1])

    sent = []

    q_row = lax.broadcasted_iota(jnp.int32, (16, 128), 0)
    q_all = jnp.where(q_row == 0, queries[0:1, :], jnp.where(q_row == 1, queries[1:2, :], 0.0))
    unit = (q_all * lax.rsqrt(jnp.sum(q_all * q_all, axis=1, keepdims=True) + 1e-06)).astype(BF16)
    stored = nt(unit, bank[...]) / DIVISOR
    mass = jnp.broadcast_to(jnp.sum(jnp.exp(stored), axis=1, keepdims=True), (16, 128))

    rs[0].wait_recv()
    own = part[pl.ds(QUARTER * right, A_TILES)].astype(F32)
    sum_a[...] = (own + via_left[...].astype(F32)).astype(BF16)
    rs[4].start()
    rs[5].start()
    rs[1].wait_recv()
    own = part[pl.ds(QUARTER * left + A_TILES, B_TILES)].astype(F32)
    sum_b[...] = (own + via_right[...].astype(F32)).astype(BF16)
    rs[6].start()


    low = lax.broadcasted_iota(jnp.int32, (2, 16, 128), 2) < 64
    pair = (13 * me) % CHIPS
    holds_a = pair < A_PAIRS
    holds_b = jnp.logical_and(pair >= A_PAIRS, pair < DATA_PAIRS)
    holds_s = pair == DATA_PAIRS
    holds_data = pair < DATA_PAIRS
    holder = pair < BACK
    held_part = jnp.where(holds_s, 2, jnp.where(holds_a, 0, 1))

    def spread(src, hold, slot, first, n):
        for i in range(n):
            p = first + (me + i) % n
            h = (5 * p) % CHIPS

            @pl.when(h != me)
            def _():
                remote(
                    src.at[p],
                    hold.at[me, core, 0],
                    hop_send.at[slot],
                    hop_recv.at[slot, me // 8],
                    (h * 2 + core, mp),
                ).start()

        @pl.when(jnp.logical_and(pair >= first, pair < first + n))
        def _():
            hold[me, core, 0] = src[pair]

    def receive(hold, slot, holds):
        def turn(side, g):
            at = pl.ds(8 * g, 8)
            x = hold[at, side, 0].reshape(256, 128).astype(F32)
            hold[at, side, 1] = pltpu.roll(x, 64, 1).astype(BF16).reshape(8, 2, 16, 128)

        def swapping(g):
            ref = hold.at[pl.ds(8 * g, 8), core, 0]
            return remote(ref, ref, pair_send.at[slot, g], pair_recv.at[slot, g], (other, mp))

        def take(i, carry):
            g = (me // 8 + 8 - i) % 8
            bytes_of(hold.at[pl.ds(8 * g, 8), core, 0], hop_recv.at[slot, g])
            swapping(g).start()
            turn(core, g)
            return carry

        def take_other(i, carry):
            g = (me // 8 + 16 - i) % 8
            bytes_of(hold.at[pl.ds(8 * g, 8), 1 - core, 0], pair_recv.at[slot, g])
            turn(1 - core, g)
            return carry

        def swapped(i, carry):
            swapping(i).wait_send()
            return carry

        @pl.when(holds)
        def _():
            lax.fori_loop(1, 8, take, 0)
            g = me // 8
            bytes_of(hold.at[pl.ds(8 * g, 7), core, 0], hop_recv.at[slot, g])
            swapping(g).start()
            turn(core, g)
            lax.fori_loop(1, 9, take_other, 0)
            lax.fori_loop(0, 8, swapped, 0)

    def deal(hold, order, out, dst, slot):
        def pick(t):
            at = 4 * t + 2 * core
            i0 = order[at]
            i1 = order[at + 1]
            x0 = hold[i0 >> 2, (i0 >> 1) & 1, i0 & 1]
            x1 = hold[i1 >> 2, (i1 >> 1) & 1, 1 - (i1 & 1)]
            return jnp.where(low, x0, x1)

        @pl.when(holder)
        def _():
            def step(i, carry):
                ts = [(me + 1 + 9 * i + u) % CHIPS for u in range(9)]
                values = [pick(t) for t in ts]
                for t, value in zip(ts, values):
                    out[t] = value
                for t in ts:
                    remote(
                        out.at[t],
                        dst.at[pair],
                        out_send.at[slot],
                        out_recv.at[slot, held_part],
                        (t * 2 + core, mp),
                    ).start()
                return carry

            lax.fori_loop(0, 7, step, 0)
            dst[pair] = pick(me)

    def arrived(dst, slot, part_of):
        start, n, holds = (
            (0, A_PAIRS, holds_a),
            (A_PAIRS, DATA_PAIRS - A_PAIRS, holds_b),
            (DATA_PAIRS, 1, holds_s),
        )[part_of]

        @pl.when(jnp.logical_not(holds))
        def _():
            bytes_of(dst.at[pl.ds(start, n)], out_recv.at[slot, part_of])

        if n > 1:

            @pl.when(holds)
            def _():
                bytes_of(dst.at[pl.ds(start, n - 1)], out_recv.at[slot, part_of])

    rs[4].wait_recv()
    rs[3].wait_recv()
    total = part[pl.ds(QUARTER * mp, A_TILES)].astype(F32)
    total = total + left_a[...].astype(F32) + right_a[...].astype(F32)
    field[0:A_PAIRS] = total.astype(BF16).reshape(A_PAIRS, 2, 16, 128)
    spread(field, hold1, 0, 0, A_PAIRS)

    for copy in (rs[2], rs[5], rs[6]):
        copy.wait_recv()
    total = part[pl.ds(QUARTER * mp + A_TILES, B_TILES)].astype(F32)
    total = total + left_b[...].astype(F32) + right_b[...].astype(F32)
    total = jnp.concatenate([total, jnp.zeros((1, 16, 128), F32)], axis=0)
    field[A_PAIRS:DATA_PAIRS] = total.astype(BF16).reshape(DATA_PAIRS - A_PAIRS, 2, 16, 128)
    spread(field, hold1, 0, A_PAIRS, DATA_PAIRS - A_PAIRS)

    def both(x):
        x = jnp.broadcast_to(x, (8, 128))
        return x + pltpu.roll(x, 64, 1)

    def offer(buf, tile, n):
        buf[mp] = tile
        copies = [
            remote(buf.at[mp], buf.at[mp], s_send.at[n, j - 1], s_recv.at[n, j - 1], (dp, (mp + j) % 4))
            for j in range(1, 4)
        ]
        for copy in copies:
            copy.start()
        return copies

    def collect(buf, n):
        for j in range(1, 4):
            bytes_of(buf.at[(mp + 4 - j) % 4], s_recv.at[n, j - 1])

    def local_stats(x):
        mean = both(jnp.sum(x, axis=0, keepdims=True)) / COUNT
        dev = x - mean[0:1]
        square = both(jnp.sum(dev * dev, axis=0, keepdims=True))
        return jnp.concatenate([mean, square], axis=0)

    def whole_stats(buf, count):
        means = [buf[q, 0:1, :] for q in range(4)]
        mean = (means[0] + means[1] + means[2] + means[3]) * 0.25
        square = jnp.zeros((1, 128), F32)
        for q in range(4):
            off = means[q] - mean
            square = square + buf[q, 8:9, :] + count * (off * off)
        return mean, square / (4.0 * count)

    def pieces(v):
        a = v.astype(BF16).astype(F32)
        b = (v - a).astype(BF16).astype(F32)
        return [a, b, v - a - b]

    x = field[0:DATA_PAIRS].reshape(32 * DATA_PAIRS, 128)[0 : 16 * QUARTER].astype(F32)
    half_count = COUNT / 2.0
    mean = jnp.sum(x, axis=0, keepdims=True) / half_count
    dev = x - mean
    square = jnp.sum(dev * dev, axis=0, keepdims=True)
    tile = jnp.concatenate([jnp.broadcast_to(mean, (8, 128)), jnp.broadcast_to(square, (8, 128))], axis=0)
    sent_stats = offer(stat1, tile, 0)
    sent += share(conv_w, 0)
    sent += share(exp_w, 1)
    sent += share(vecs, 2)
    receive(hold1, 0, holds_data)
    collect(stat1, 0)
    mean, var = whole_stats(stat1, half_count)

    def stat_tile(values):
        tile = jnp.zeros((16, 128), F32)
        for r, v in enumerate(values):
            tile = jnp.where(q_row == r, v, tile)
        return jnp.concatenate([tile, jnp.zeros((16, 128), F32)], axis=0).astype(BF16).reshape(2, 16, 128)

    field[DATA_PAIRS] = stat_tile(pieces(mean) + pieces(var))
    spread(field, hold1, 0, DATA_PAIRS, 1)
    receive(hold1, 0, holds_s)

    deal(hold1, perm, out1, group, 0)
    for n, buf in enumerate((conv_w, exp_w, vecs)):
        shared(buf, sent, n)
    conv_blocks = []
    for dy in range(3):
        w = jnp.concatenate([conv_w[q, dy] for q in range(4)] * 2, axis=0).astype(F32)
        conv_blocks.append(jnp.where(same, w, 0.0).astype(BF16))
    vec_all = vecs[0] + vecs[1] + vecs[2] + vecs[3]
    arrived(group, 0, 0)
    arrived(group, 0, 1)
    halos = [
        remote(group.at[pl.ds(0, 2)], halo_bottom, halo_send.at[0], halo_recv.at[0], to_l),
        remote(group.at[pl.ds(DATA_PAIRS - 3, 3)], halo_top, halo_send.at[1], halo_recv.at[1], to_r),
    ]
    for copy in halos:
        copy.start()
    arrived(group, 0, 2)


    marks = group[DATA_PAIRS, 0].astype(F32)
    mean_i = marks[0:1] + marks[1:2] + marks[2:3]
    var_i = marks[3:4] + marks[4:5] + marks[5:6]
    mean = (both(mean_i) * 0.5)[0:1]
    off = mean_i - mean
    var = (both(var_i + off * off) * 0.5)[0:1]
    scale = lax.rsqrt(var + 1e-05)

    def norm1(tiles):
        x = tiles.astype(F32)
        return jnp.maximum((x - mean) * scale * vec_all[0:1] + vec_all[1:2], 0.0)

    inner = norm1(group[0:DATA_PAIRS].reshape(32 * DATA_PAIRS, 128)[0 : 16 * QUARTER]).reshape(LINES, SIDE, 128)
    for copy in halos:
        copy.wait_recv()
    top = norm1(halo_top[...].reshape(96, 128))[24:80]
    bottom = norm1(halo_bottom[...].reshape(64, 128))[0:SIDE]
    top = jnp.where(jnp.full((SIDE, 128), mp, jnp.int32) == 0, 0.0, top).reshape(1, SIDE, 128)
    bottom = jnp.where(jnp.full((SIDE, 128), mp, jnp.int32) == 3, 0.0, bottom).reshape(1, SIDE, 128)
    first = jnp.concatenate([top, inner, bottom], axis=0)
    first = jnp.concatenate([first, jnp.zeros((LINES + 2, COLS - SIDE, 128), F32)], axis=1)
    first = first.reshape((LINES + 2) * COLS, 128)

    wide = jnp.concatenate(
        [
            pltpu.roll(first, 1, 0).astype(BF16),
            first.astype(BF16),
            pltpu.roll(first, (LINES + 2) * COLS - 1, 0).astype(BF16),
        ],
        axis=1,
    )
    n_out = LINES * COLS
    spatial = nt(wide[0:n_out], conv_blocks[0])
    spatial = spatial + nt(wide[COLS : COLS + n_out], conv_blocks[1])
    spatial = spatial + nt(wide[2 * COLS : 2 * COLS + n_out], conv_blocks[2])
    spatial = spatial.reshape(LINES, COLS, 128)[:, :SIDE, :].reshape(16 * QUARTER, 128)

    sent_stats += offer(stat2, local_stats(spatial), 1)
    collect(stat2, 1)
    mean, var = whole_stats(stat2, COUNT)
    second = jnp.maximum((spatial - mean) * lax.rsqrt(var + 1e-05) * vec_all[2:3] + vec_all[3:4], 0.0).astype(BF16)
    padded = jnp.concatenate([second, jnp.zeros((16, 128), BF16)], axis=0)
    mid[0:DATA_PAIRS] = padded.reshape(DATA_PAIRS, 2, 16, 128)
    spread(mid, hold2, 1, 0, DATA_PAIRS)

    copies3 = []
    for q in range(4):
        stat3s[q] = local_stats(nt(second, diagonal(exp_w[q].astype(F32))))
    for j in range(1, 4):
        q = (mp + j) % 4
        copy = remote(stat3s.at[q], stat3.at[mp], s_send.at[2, j - 1], s_recv.at[2, j - 1], (dp, q))
        copy.start()
        copies3.append(copy)
    stat3[mp] = stat3s[mp]
    sent_stats += copies3
    receive(hold2, 1, holds_data)
    collect(stat3, 2)
    mean, var = whole_stats(stat3, COUNT)
    mid[DATA_PAIRS] = stat_tile(pieces(mean) + pieces(lax.rsqrt(var + 1e-05)))
    spread(mid, hold2, 1, DATA_PAIRS, 1)
    receive(hold2, 1, holds_s)
    deal(hold2, inv, out2, home, 1)

    def a_of(q):
        return second_all.at[pl.ds(QUARTER * q, A_TILES)]

    def b_of(q):
        return second_all.at[pl.ds(QUARTER * q + A_TILES, B_TILES)]

    ag = [
        remote(a_of(mp), a_of(mp), ag_send.at[0], ag_recv.at[0], to_r),
        remote(a_of(mp), a_of(mp), ag_send.at[1], ag_recv.at[1], to_l),
        remote(b_of(mp), b_of(mp), ag_send.at[2], ag_recv.at[2], to_l),
        remote(b_of(mp), b_of(mp), ag_send.at[3], ag_recv.at[3], to_r),
        remote(a_of(left), a_of(left), ag_send.at[4], ag_recv.at[4], to_r),
        remote(b_of(right), b_of(right), ag_send.at[5], ag_recv.at[5], to_l),
    ]
    arrived(home, 1, 0)
    second_all[pl.ds(QUARTER * mp, A_TILES)] = home[0:A_PAIRS].reshape(A_TILES, 16, 128)
    ag[0].start()
    arrived(home, 1, 1)
    second_all[pl.ds(QUARTER * mp + A_TILES, B_TILES)] = home[A_PAIRS:DATA_PAIRS].reshape(B_TILES + 1, 16, 128)[0:B_TILES]
    ag[2].start()
    ag[3].start()
    ag[1].start()
    bytes_of(a_of(left), ag_recv.at[0])
    ag[4].start()
    bytes_of(b_of(right), ag_recv.at[2])
    ag[5].start()
    arrived(home, 1, 2)

    identity = jnp.where(
        lax.broadcasted_iota(jnp.int32, (128, 128), 0) == lax.broadcasted_iota(jnp.int32, (128, 128), 1),
        1.0,
        0.0,
    ).astype(BF16)
    columns = nt(identity, home[DATA_PAIRS, 0])
    mean_c = columns[:, 0:1] + columns[:, 1:2] + columns[:, 2:3]
    scale_c = columns[:, 3:4] + columns[:, 4:5] + columns[:, 5:6]

    def expand(block, lanes):
        v = nt(we_block, block)
        third = ((v - mean_c) * scale_c * gain_c + shift_c).astype(BF16).astype(F32)
        f = jnp.maximum(third + img[:, lanes].astype(F32), 0.0).astype(BF16)
        feat[:, lanes] = f
        return f.astype(F32)

    def expand_at(i, pooled):
        j = ((QUARTER * far + QUARTER - 1) // 32 + 1 + i) % 6
        block = second_all[pl.ds(32 * j, 32)].reshape(512, 128)
        f = expand(block, pl.ds(pl.multiple_of(512 * j, 512), 512))
        return pooled + (f[:, 0:128] + f[:, 128:256] + f[:, 256:384] + f[:, 384:512])

    bytes_of(a_of(right), ag_recv.at[1])
    bytes_of(b_of(left), ag_recv.at[3])
    pooled = jnp.zeros((128, 128), F32)
    for i in range(3):
        pooled = expand_at(i, pooled)
    bytes_of(a_of(far), ag_recv.at[4])
    bytes_of(b_of(far), ag_recv.at[5])
    for i in range(3, 6):
        pooled = expand_at(i, pooled)
    rest = expand(second_all[192:196].reshape(64, 128), slice(3072, 3136))
    write = pltpu.make_async_copy(feat, feat_hbm, feat_sem)
    write.start()
    pooled = jnp.sum(pooled, axis=1, keepdims=True) + jnp.sum(rest, axis=1, keepdims=True)
    pooled = pooled / float(PIXELS)

    proj2 = jnp.concatenate([proj[...], proj[...]], axis=0).astype(F32)
    terms = pooled * proj2
    e0 = jnp.sum(terms[0:64], axis=0, keepdims=True)
    e1 = jnp.sum(terms[64:128], axis=0, keepdims=True)
    row8 = lax.broadcasted_iota(jnp.int32, (8, 128), 0)
    top = jnp.where(row8 == 0, e0, jnp.where(row8 == 1, e1, 0.0))
    emb[core, mp] = jnp.concatenate([top, mass[0:8]], axis=0)
    mine = emb.at[core, mp]
    e_copies = []
    for j in range(1, 4):
        e_copies.append(remote(mine, mine, e_send.at[j], e_recv.at[j], (dp, (mp + j) % 4)))
    for j in range(4):
        e_copies.append(remote(mine, mine, e_send.at[4 + j], e_recv.at[4 + j], (other, (mp + j) % 4)))
    for copy in e_copies:
        copy.start()
    for j in range(1, 4):
        bytes_of(emb.at[core, (mp + 4 - j) % 4], e_recv.at[j])
    for j in range(4):
        bytes_of(emb.at[1 - core, (mp + 4 - j) % 4], e_recv.at[4 + j])

    key_tile = jnp.zeros((16, 128), F32)
    for cc in range(2):
        e = emb[cc, 0, 0:8] + emb[cc, 1, 0:8] + emb[cc, 2, 0:8] + emb[cc, 3, 0:8]
        key = e * lax.rsqrt(jnp.sum(e * e, axis=1, keepdims=True) + 1e-06)
        for b in range(2):
            here = q_row == 4 * (me % 4) + 2 * cc + b
            key_tile = jnp.where(here, key[b : b + 1], key_tile)
    queue = emb[core, 0, 8:16] + emb[core, 1, 8:16] + emb[core, 2, 8:16] + emb[core, 3, 8:16]
    z = me % 8
    slab = me // 8
    keys1[z] = key_tile.astype(BF16)
    k_copies = []
    for j in range(1, 8):
        h = slab * 8 + (z + j) % 8
        k_copies.append(remote(keys1.at[z], keys1.at[z], k_send.at[0, j], k_recv.at[0, j], (h * 2 + core, mp)))
    for copy in k_copies:
        copy.start()
    for j in range(1, 8):
        bytes_of(keys1.at[(z + 8 - j) % 8], k_recv.at[0, j])
    keys2[slab] = jnp.sum(keys1[...].astype(F32).reshape(2, 4, 16, 128), axis=1).astype(BF16)
    k_copies2 = []
    for j in range(1, 8):
        h = (me + 8 * j) % CHIPS
        k_copies2.append(
            remote(keys2.at[slab], keys2.at[slab], k_send.at[1, j], k_recv.at[1, j], (h * 2 + core, mp))
        )
    for copy in k_copies2:
        copy.start()
    for j in range(1, 8):
        bytes_of(keys2.at[(slab + 8 - j) % 8], k_recv.at[1, j])
    every = keys2[...].reshape(256, 128)
    score = (nt(unit, every) / DIVISOR)[0:8]
    score_out[...] = score[0:2]
    lane = lax.broadcasted_iota(jnp.int32, (8, 256), 1)
    row = lax.broadcasted_iota(jnp.int32, (8, 256), 0)
    matched = jnp.sum(jnp.where(lane == 2 * dp + row, score, 0.0), axis=1, keepdims=True)
    mass_all = jnp.sum(jnp.exp(score), axis=1, keepdims=True) + queue[:, 0:1]
    losses = jnp.broadcast_to(jnp.log(mass_all) - matched, (8, 128))
    lane8 = lax.broadcasted_iota(jnp.int32, (8, 128), 1)
    loss_out[...] = jnp.sum(jnp.where(row8 == lane8, losses, 0.0), axis=0, keepdims=True)[:, 0:2]

    write.wait()
    for copy in rs + sent + sent_stats + ag + halos + e_copies + k_copies + k_copies2:
        copy.wait_send()
    for slot, (src, out) in enumerate(((field, out1), (mid, out2))):

        @pl.when(holder)
        def _():
            bytes_of(src.at[pl.ds(0, BACK - 1)], hop_send.at[slot])
            bytes_of(out.at[pl.ds(0, CHIPS - 1)], out_send.at[slot])

        @pl.when(jnp.logical_not(holder))
        def _():
            bytes_of(src, hop_send.at[slot])


def on_device(
    images,
    permutation,
    inverse,
    reduce_weight,
    reduce_gain,
    reduce_shift,
    spatial_weight,
    spatial_gain,
    spatial_shift,
    expand_weight,
    expand_gain,
    expand_shift,
    projection,
    queries,
    dictionary_bank,
):
    cw = jnp.transpose(spatial_weight, (2, 3, 0, 1))
    rows = [
        v.reshape(1, -1)
        for v in (reduce_gain, reduce_shift, spatial_gain, spatial_shift, expand_gain, expand_shift)
    ]

    vmem = pl.BlockSpec(memory_space=pltpu.VMEM)
    smem = pl.BlockSpec(memory_space=pltpu.SMEM)
    dma = pltpu.SemaphoreType.DMA
    feat, score, loss = pl.pallas_call(
        kernel,
        out_shape=(
            jax.ShapeDtypeStruct((128, PIXELS), BF16),
            jax.ShapeDtypeStruct((2, 256), F32),
            jax.ShapeDtypeStruct((1, 2), F32),
        ),
        in_specs=[smem, smem, pl.BlockSpec(memory_space=pl.ANY)] + [vmem] * 12,
        out_specs=(pl.BlockSpec(memory_space=pl.ANY), vmem, vmem),
        scratch_shapes=[
            pltpu.VMEM((128, PIXELS), BF16),
            pltpu.VMEM((128, PIXELS), BF16),
            pltpu.VMEM((4 * QUARTER, 16, 128), BF16),
            pltpu.VMEM((QUARTER, 16, 128), BF16),
            pltpu.VMEM((QUARTER, 16, 128), BF16),
            pltpu.VMEM((A_TILES, 16, 128), BF16),
            pltpu.VMEM((B_TILES, 16, 128), BF16),
            pltpu.VMEM((A_TILES, 16, 128), BF16),
            pltpu.VMEM((B_TILES, 16, 128), BF16),
            pltpu.VMEM((4, 3, 16, 384), BF16),
            pltpu.VMEM((4, 64, 128), BF16),
            pltpu.VMEM((4, 8, 128), F32),
            pltpu.VMEM((BACK, 2, 16, 128), BF16),
            pltpu.VMEM((CHIPS, 2, 2, 2, 16, 128), BF16),
            pltpu.VMEM((CHIPS, 2, 16, 128), BF16),
            pltpu.VMEM((BACK, 2, 16, 128), BF16),
            pltpu.VMEM((4, 16, 128), F32),
            pltpu.VMEM((4, 16, 128), F32),
            pltpu.VMEM((4, 16, 128), F32),
            pltpu.VMEM((4, 16, 128), F32),
            pltpu.VMEM((BACK, 2, 16, 128), BF16),
            pltpu.VMEM((CHIPS, 2, 2, 2, 16, 128), BF16),
            pltpu.VMEM((CHIPS, 2, 16, 128), BF16),
            pltpu.VMEM((BACK, 2, 16, 128), BF16),
            pltpu.VMEM((4 * QUARTER, 16, 128), BF16),
            pltpu.VMEM((2, 4, 16, 128), F32),
            pltpu.VMEM((8, 16, 128), BF16),
            pltpu.VMEM((8, 2, 16, 128), BF16),
            pltpu.VMEM((3, 2, 16, 128), BF16),
            pltpu.VMEM((2, 2, 16, 128), BF16),
            dma,
            dma,
            dma((7,)),
            dma((7,)),
            dma((3, 3)),
            dma((3, 3)),
            dma((3, 3)),
            dma((3, 3)),
            dma((2,)),
            dma((2, 8)),
            dma((2,)),
            dma((2, 3)),
            dma((2,)),
            dma((2,)),
            dma((2, 8)),
            dma((2, 8)),
            dma((6,)),
            dma((6,)),
            dma((8,)),
            dma((8,)),
            dma((2, 8)),
            dma((2, 8)),
        ],
        compiler_params=pltpu.CompilerParams(
            collective_id=0, has_side_effects=True, vmem_limit_bytes=63 * 1024 * 1024
        ),
        cost_estimate=pl.CostEstimate(
            flops=2 * 3136 * 128 * 128 * 4, bytes_accessed=2 * 128 * 3136 * 2, transcendentals=0
        ),
    )(
        permutation,
        inverse,
        images.reshape(128, PIXELS),
        reduce_weight,
        cw,
        expand_weight,
        *rows,
        projection,
        queries,
        dictionary_bank,
    )
    return feat.reshape(images.shape), score, loss.reshape(2)


def solution(mesh):
    placed = (
        P("dp", "mp", None),
        P(),
        P(),
        P(None, "mp"),
        P("mp"),
        P("mp"),
        P("mp", None, None, None),
        P("mp"),
        P("mp"),
        P("mp", None),
        P("mp"),
        P("mp"),
        P("mp", None),
        P("dp", None),
        P("mp", None),
    )
    return jax.shard_map(
        on_device,
        mesh=mesh,
        in_specs=placed,
        out_specs=(P("dp", "mp", None), P("dp", None), P("dp")),
        check_vma=False,
    )
```
